256 devices in a mesh: node: 16 (over y, x), feat: 16 (over z, core).
Axes of the slice: x: 4, y: 4, z: 8, core: 2. Of those that a mesh axis runs over, the one named last changes fastest.
Arguments:
- features: bfloat16 [131072, 4096], P('node', 'feat'), may hold values from -6 to 6
- adjacency: bfloat16 [4096, 128, 128], P('node'), may hold values from 0 to 0.039794922
- target_block: int32 [4096], P('node'), may hold values from 0 to 127
- source_block: int32 [4096], P('node'), may hold values from 0 to 63
- block_count: int32 [16], P('node'), may hold values from 64 to 256, as said below
- layer_one: bfloat16 [4096, 256], P('feat'), may hold values from -0.09375 to 0.09375
- bias_one: float32 [256], replicated, may hold values from -3 to 3
- self_weight: bfloat16 [256, 172], replicated, may hold values from -0.375 to 0.375
- neigh_weight: bfloat16 [256, 172], replicated, may hold values from -0.375 to 0.375
- bias_two: float32 [172], replicated, may hold values from -4 to 4
- seed_ids: int32 [8192], P(('node', 'feat')), may hold values from 0 to 63
- neighbor_ids: int32 [8192, 8], P(('node', 'feat')), may hold values from 0 to 63
Outputs:
- logits: float32 [8192, 172], P(('node', 'feat'))
The draws below stay inside these ranges and needn't reach their ends.
Inputs may be any that keep to these rules, and one draw needn't show every extreme that they name: Only the first block_count[n] slots of node shard n are live; some node shard has all 256 live.
All inputs are finite; a program needn't handle non-finite values.
Results may differ from the reference program's by a relative error of at most 0.0028.
Values sent between devices are 32-bit elements; how exact they have to be, the bound alone decides.
No kernel may reach another device: no remote copies, remote signals or barrier semaphores. Data moves between devices by JAX's collectives and lax.ppermute only.
A program may use at most 192 MiB of HBM per device.

```python
import jax
import jax.numpy as jnp
from jax import lax

F = 4096
H = 256
C = 172
BLK = 128
FAN = 8
NODE_DEV = 8192
MAXB = 256
T_DEV = 64
S_DEV = 32
NODES = 131072
TARGETS = 16384
SEEDS = 8192
BLOCKS = 4096
N_NODE = 16


def draw_block_count(key, part):
    key = jax.random.fold_in(key, 11)
    counts = jax.random.randint(key, (N_NODE,), MAXB // 4, MAXB + 1)
    fullest = jax.random.randint(jax.random.fold_in(key, 1), (), 0, N_NODE)
    return jnp.where(jnp.arange(N_NODE) == fullest, MAXB, counts).astype(jnp.int32)


def draw_target_block(key, part):
    key = jax.random.fold_in(key, 12)
    values = jax.random.randint(key, (BLOCKS,), 0, TARGETS // BLK)
    topmost = jax.random.randint(jax.random.fold_in(key, 1), (), 0, BLOCKS)
    return jnp.where(jnp.arange(BLOCKS) == topmost, TARGETS // BLK - 1, values).astype(jnp.int32)


def draw_source_block(key, part):
    key = jax.random.fold_in(key, 13)
    values = jax.random.randint(key, (BLOCKS,), 0, NODE_DEV // BLK)
    topmost = jax.random.randint(jax.random.fold_in(key, 1), (), 0, BLOCKS)
    return jnp.where(jnp.arange(BLOCKS) == topmost, NODE_DEV // BLK - 1, values).astype(jnp.int32)


def touch_ends(entries, rng, least, largest):
    dims = entries.shape
    spot = [jax.random.randint(jax.random.fold_in(rng, axis), (), 0, dims[axis]) for axis in range(len(dims))]
    entries = entries.at[tuple(spot)].set(least)
    longest = dims.index(max(dims))
    spot[longest] = (spot[longest] + 1) % dims[longest]
    return entries.at[tuple(spot)].set(largest)


def levels(stream_key, dims, shards, smallest, top_value):
    level = 1.0
    for position, blocks in shards:
        heights = jax.random.uniform(jax.random.fold_in(jax.random.fold_in(stream_key, 6), position), (blocks,), jnp.float32, smallest / len(shards), top_value / len(shards))
        level = level * jnp.repeat(jnp.exp(heights), dims[position] // blocks).reshape((-1,) + (1,) * (len(dims) - 1 - position))
    return level


def gaussian(own_key, dims, spread, most, cuts=(), kind=jnp.bfloat16):
    level = levels(own_key, dims, cuts, -0.22, 0.18) if cuts else 1.0
    values = jax.random.normal(own_key, dims, jnp.float32) * spread * level
    return jnp.minimum(jnp.maximum(values, -most), most).astype(kind)


def setup_inputs(seed: int = 0) -> dict:
    splits = jax.random.split(jax.random.key(seed), 13)
    return {
        "features": gaussian(splits[0], (NODES, F), 1.0, 6.0, ((0, 16), (1, 16))),
        "adjacency": jnp.clip(0.039794922 * jax.random.uniform(splits[1], (BLOCKS, BLK, BLK), jnp.float32) ** levels(splits[1], (BLOCKS, BLK, BLK), ((0, 16),), -0.2, 0.2), 0.0, 0.039794922).astype(jnp.bfloat16),
        "target_block": draw_target_block(jax.random.fold_in(splits[12], 71), 0),
        "source_block": draw_source_block(jax.random.fold_in(splits[12], 71), 0),
        "block_count": draw_block_count(jax.random.fold_in(splits[12], 71), 0),
        "layer_one": gaussian(splits[5], (F, H), F ** -0.5, 0.09375, ((0, 16),)),
        "bias_one": gaussian(splits[6], (H,), 0.5, 3.0, (), jnp.float32),
        "self_weight": gaussian(splits[7], (H, C), H ** -0.5, 0.375),
        "neigh_weight": gaussian(splits[8], (H, C), H ** -0.5, 0.375),
        "bias_two": gaussian(splits[9], (C,), 1.0, 4.0, (), jnp.float32),
        "seed_ids": touch_ends(jax.random.randint(splits[10], (SEEDS,), 0, T_DEV), jax.random.fold_in(splits[10], 1), 0, T_DEV - 1).astype(jnp.int32),
        "neighbor_ids": touch_ends(jax.random.randint(splits[11], (SEEDS, FAN), 0, T_DEV), jax.random.fold_in(splits[11], 1), 0, T_DEV - 1).astype(jnp.int32),
    }


def reference(features, adjacency, target_block, source_block, block_count, layer_one, bias_one, self_weight, neigh_weight, bias_two, seed_ids, neighbor_ids):
    feature_blocks = features.reshape(N_NODE, NODE_DEV // BLK, BLK, F)
    adjacency_blocks = adjacency.reshape(N_NODE, MAXB, BLK, BLK)
    target_lists = target_block.reshape(N_NODE, MAXB)
    source_lists = source_block.reshape(N_NODE, MAXB)

    def one_shard(running, pieces):
        shard_rows, shard_weights, shard_targets, shard_sources, shard_count = pieces
        gathered = shard_rows[shard_sources].astype(jnp.float32)
        products = jnp.einsum("bij,bjf->bif", shard_weights.astype(jnp.float32), gathered)
        live_mask = (jnp.arange(MAXB, dtype=jnp.int32) < shard_count).astype(jnp.float32)
        placed = jnp.zeros((TARGETS // BLK, BLK, F), jnp.float32).at[shard_targets].add(products * live_mask[:, None, None])
        aggregated = placed.reshape(TARGETS, F).astype(jnp.bfloat16)
        return running + jnp.dot(aggregated, layer_one, preferred_element_type=jnp.float32), None

    hidden_sum, _ = lax.scan(one_shard, jnp.zeros((TARGETS, H), jnp.float32), (feature_blocks, adjacency_blocks, target_lists, source_lists, block_count))
    hidden_one = jnp.maximum(hidden_sum + bias_one[None, :], 0.0).astype(jnp.bfloat16)
    offsets = (jnp.arange(SEEDS, dtype=jnp.int32) // S_DEV) * T_DEV
    self_rows = hidden_one[offsets + seed_ids]
    neigh_rows = hidden_one[offsets[:, None] + neighbor_ids].astype(jnp.float32)
    neigh_mean = jnp.mean(neigh_rows, axis=1).astype(jnp.bfloat16)
    logits = jnp.dot(self_rows, self_weight, preferred_element_type=jnp.float32) + jnp.dot(neigh_mean, neigh_weight, preferred_element_type=jnp.float32)
    return logits + bias_two[None, :]
```

```python
import functools

import jax
import jax.numpy as jnp
from jax import lax
from jax.experimental import pallas as pl
from jax.experimental.pallas import tpu as pltpu
from jax.sharding import PartitionSpec as P

T_DEV = 64
NT = (((1,), (1,)), ((), ()))


def project_kernel(where, layer_one, features, *refs):
    *outs, ordered = refs
    chips = where[2]
    width = outs[0].shape[1]
    hidden = layer_one.shape[1]

    @pl.when(pl.program_id(0) == 0)
    def _():
        row = lax.broadcasted_iota(jnp.int32, (hidden, hidden), 0)
        column = lax.broadcasted_iota(jnp.int32, (hidden, hidden), 1)
        half = hidden // 2
        other = (row < half).astype(jnp.int32)
        place = (row % half) // width
        hop = (place + 1) // 2
        hop = chips // 2 + jnp.where(place % 2 == 1, -hop, hop)
        chip = (where[0] + hop) % chips
        core = (where[1] + other) % 2
        wanted = (chip * 2 + core) * width + row % width
        pick = (column == wanted).astype(jnp.bfloat16)
        ordered[...] = lax.dot_general(
            pick, layer_one[...], NT, preferred_element_type=jnp.float32
        ).astype(jnp.bfloat16)

    product = lax.dot_general(ordered[...], features[...], NT, preferred_element_type=jnp.float32)
    at = 0
    for out in outs:
        for k in range(out.shape[0]):
            out[k] = product[at : at + width]
            at += width


def project(where, layer_one, features, chips, width):
    rows, columns = features.shape
    hidden = layer_one.shape[1]
    tile = min(1024, rows)
    groups = [1] + [2] * (chips // 2 - 1) + [1]
    shapes = [jax.ShapeDtypeStruct((g, width, rows), jnp.float32) for g in groups] * 2
    return pl.pallas_call(
        project_kernel,
        grid_spec=pltpu.PrefetchScalarGridSpec(
            num_scalar_prefetch=1,
            grid=(rows // tile,),
            in_specs=[
                pl.BlockSpec((columns, hidden), lambda i, w: (0, 0)),
                pl.BlockSpec((tile, columns), lambda i, w: (i, 0)),
            ],
            out_specs=[pl.BlockSpec((g, width, tile), lambda i, w: (0, 0, i)) for g in groups] * 2,
            scratch_shapes=[pltpu.VMEM((hidden, columns), jnp.bfloat16)],
        ),
        out_shape=shapes,
        name="project",
        compiler_params=pltpu.CompilerParams(vmem_limit_bytes=24 * 2**20),
        cost_estimate=pl.CostEstimate(
            flops=2 * rows * columns * hidden,
            bytes_accessed=rows * columns * 2 + rows * hidden * 4,
            transcendentals=0,
        ),
    )(where, layer_one, features)


def blocks_kernel(target, source, count, own, paired, forward, backward, adjacency, out, held):
    step = pl.program_id(0)
    group = adjacency.shape[0]
    size = adjacency.shape[1]

    @pl.when(step == 0)
    def _():
        out[...] = jnp.zeros_like(out)
        for b in range(held.shape[0]):
            at = slice(b * size, (b + 1) * size)
            held[b] = (
                (own[0, :, at] + paired[0, :, at]) + (forward[0, :, at] + backward[0, :, at])
            ).astype(held.dtype)

    first = step * group
    live = count[0]

    @pl.when(first + group <= live)
    def _():
        products = []
        for k in range(group):
            products.append(
                lax.dot_general(
                    held[source[first + k]], adjacency[k], NT, preferred_element_type=jnp.float32
                )
            )
        for k in range(group):
            out[target[first + k]] += products[k]

    @pl.when((first < live) & (first + group > live))
    def _():
        for k in range(group):

            @pl.when(first + k < live)
            def _():
                out[target[first + k]] += lax.dot_general(
                    held[source[first + k]], adjacency[k], NT, preferred_element_type=jnp.float32
                )


def blocks(target, source, count, own, paired, forward, backward, adjacency, target_blocks):
    slots, size, _ = adjacency.shape
    width, rows = own.shape[1:]
    group = 16

    def last_live(i, t, s, c):
        return jnp.minimum(i, (c[0] - 1) // group), 0, 0

    whole = pl.BlockSpec((1, width, rows), lambda i, t, s, c: (0, 0, 0))
    return pl.pallas_call(
        blocks_kernel,
        grid_spec=pltpu.PrefetchScalarGridSpec(
            num_scalar_prefetch=3,
            grid=(slots // group,),
            in_specs=[whole] * 4 + [pl.BlockSpec((group, size, size), last_live)],
            out_specs=pl.BlockSpec((target_blocks, width, size), lambda i, t, s, c: (0, 0, 0)),
            scratch_shapes=[pltpu.VMEM((rows // size, width, size), jnp.bfloat16)],
        ),
        out_shape=jax.ShapeDtypeStruct((target_blocks, width, size), jnp.float32),
        name="blocks",
        compiler_params=pltpu.CompilerParams(vmem_limit_bytes=24 * 2**20),
        cost_estimate=pl.CostEstimate(
            flops=2 * slots * size * size * width,
            bytes_accessed=slots * size * size * 2,
            transcendentals=0,
        ),
    )(target, source, count, own, paired, forward, backward, adjacency)


def second_kernel(where, sums, bias_one, self_weight, neigh_weight, bias_two, seeds, neighbors, out):
    hidden = jnp.maximum(sums[...] + bias_one[...], 0.0).astype(jnp.bfloat16)
    count, fan = neighbors.shape
    positions = lax.broadcasted_iota(jnp.int32, (count, hidden.shape[1]), 1) - where[1] * T_DEV
    pick_self = (positions == seeds[...]).astype(jnp.bfloat16)
    tally = jnp.zeros(positions.shape, jnp.float32)
    for k in range(fan):
        tally += (positions == neighbors[:, k : k + 1]).astype(jnp.float32)
    weights_mean = (tally / fan).astype(jnp.bfloat16)
    self_rows = lax.dot_general(pick_self, hidden, NT, preferred_element_type=jnp.float32)
    neigh_mean = lax.dot_general(weights_mean, hidden, NT, preferred_element_type=jnp.float32)
    out[...] = (
        jnp.dot(
            self_rows.astype(jnp.bfloat16), self_weight[...], preferred_element_type=jnp.float32
        )
        + jnp.dot(
            neigh_mean.astype(jnp.bfloat16), neigh_weight[...], preferred_element_type=jnp.float32
        )
        + bias_two[...]
    )


def second(where, sums, bias_one, self_weight, neigh_weight, bias_two, seeds, neighbors):
    vmem = pl.BlockSpec(memory_space=pltpu.VMEM)
    return pl.pallas_call(
        second_kernel,
        in_specs=[pl.BlockSpec(memory_space=pltpu.SMEM)] + [vmem] * 7,
        out_specs=vmem,
        out_shape=jax.ShapeDtypeStruct((seeds.shape[0], bias_two.shape[0]), jnp.float32),
        name="second",
        compiler_params=pltpu.CompilerParams(vmem_limit_bytes=16 * 2**20),
    )(
        where,
        sums,
        bias_one[:, None],
        self_weight,
        neigh_weight,
        bias_two[None, :],
        seeds[:, None],
        neighbors,
    )


def on_device(
    features,
    adjacency,
    target_block,
    source_block,
    block_count,
    layer_one,
    bias_one,
    self_weight,
    neigh_weight,
    bias_two,
    seed_ids,
    neighbor_ids,
):
    size = adjacency.shape[1]
    node_count = lax.axis_size("node")
    feat_count = lax.axis_size("feat")
    chips = feat_count // 2
    hidden = layer_one.shape[1]
    width = hidden // feat_count
    target_blocks = T_DEV * node_count * feat_count // size
    feat = lax.axis_index("feat")
    where = jnp.stack([feat // 2, feat % 2, jnp.int32(chips)]).astype(jnp.int32)

    pair = [(i, i ^ 1) for i in range(feat_count)]
    up = [(i, (i + 2) % feat_count) for i in range(feat_count)]
    down = [((i + 2) % feat_count, i) for i in range(feat_count)]

    def send(value, route):
        return lax.ppermute(value, "feat", route)

    *parts, = project(where, layer_one, features, chips, width)
    groups = len(parts) // 2
    paired = [send(part, pair) for part in parts[:groups]]
    kept = parts[groups:]

    half = width // 2
    opposite = kept[0][0] + paired[0][0]
    forward = send(opposite[:half], up)
    backward = send(opposite[half:], down)
    for g in range(1, groups - 1):
        onward = kept[g][0] + paired[g][0]
        back = kept[g][1] + paired[g][1]
        if g == 1:
            onward = jnp.concatenate([onward[:half] + forward, onward[half:]])
            back = jnp.concatenate([back[:half], back[half:] + backward])
        else:
            onward = onward + forward
            back = back + backward
        forward = send(onward, up)
        backward = send(back, down)

    partial = blocks(
        target_block,
        source_block,
        block_count,
        kept[-1],
        paired[-1],
        forward[None],
        backward[None],
        adjacency,
        target_blocks,
    )

    partial = partial.reshape(node_count, chips, width, size)
    summed = jnp.sum(lax.all_to_all(partial, "node", 0, 0), axis=0)
    doubled = jnp.broadcast_to(summed[:, None], (chips, 2, width, size))
    sums = lax.all_to_all(doubled.reshape(feat_count, width, size), "feat", 0, 0)
    return second(
        where,
        sums.reshape(hidden, size),
        bias_one,
        self_weight,
        neigh_weight,
        bias_two,
        seed_ids,
        neighbor_ids,
    )


def solution(mesh):
    placed = (
        P("node", "feat"),
        P("node", None, None),
        P("node"),
        P("node"),
        P("node"),
        P("feat", None),
        P(),
        P(),
        P(),
        P(),
        P(("node", "feat")),
        P(("node", "feat"), None),
    )
    return jax.shard_map(
        on_device, mesh=mesh, in_specs=placed, out_specs=P(("node", "feat"), None), check_vma=False
    )
```

```python
import jax
import jax.numpy as jnp
from jax import lax
from jax.experimental import pallas as pl
from jax.experimental.pallas import tpu as pltpu
from jax.sharding import PartitionSpec as P

T_DEV = 64
NT = (((1,), (1,)), ((), ()))


VMEM = pl.BlockSpec(memory_space=pltpu.VMEM)
SMEM = pl.BlockSpec(memory_space=pltpu.SMEM)


def project_kernel(where, layer_one, features, *outs):
    chips, streams = 8, 2
    strip = outs[0].shape[1]
    width = streams * strip
    hidden = layer_one.shape[1]
    row = lax.broadcasted_iota(jnp.int32, (hidden, hidden), 0)
    column = lax.broadcasted_iota(jnp.int32, (hidden, hidden), 1)
    half = hidden // 2
    core = (where[1] + (row < half).astype(jnp.int32)) % 2
    place = (row % half) // width
    hop = (place + 1) // 2
    hop = chips // 2 + jnp.where(place % 2 == 1, -hop, hop)
    chip = (where[0] + hop) % chips
    wanted = (chip * 2 + core) * width + row % width
    pick = (column == wanted).astype(jnp.bfloat16)
    ordered = lax.dot_general(
        pick, layer_one[...], NT, preferred_element_type=jnp.float32
    ).astype(jnp.bfloat16)

    tiles = 16
    tile = features.shape[0] // tiles
    for i in range(tiles):
        rows = features[i * tile : (i + 1) * tile]
        product = lax.dot_general(ordered, rows, NT, preferred_element_type=jnp.float32)
        side, at = divmod(i, tiles // 2)
        take = 0
        for out in outs:
            for k in range(out.shape[0] // 2):
                out[2 * k + side, :, at * tile : (at + 1) * tile] = product[take : take + strip]
                take += strip


def project(where, layer_one, features):
    rows, columns = features.shape
    hidden = layer_one.shape[1]
    strip = hidden // 32
    shapes = [
        jax.ShapeDtypeStruct((4 * hops, strip, rows // 2), jnp.float32) for hops in (1, 2, 5)
    ] * 2
    return pl.pallas_call(
        project_kernel,
        in_specs=[SMEM, VMEM, VMEM],
        out_specs=[VMEM] * 6,
        out_shape=shapes,
        name="project",
        compiler_params=pltpu.CompilerParams(vmem_limit_bytes=8 * 2**20),
        cost_estimate=pl.CostEstimate(
            flops=2 * rows * columns * hidden,
            bytes_accessed=rows * columns * 2 + rows * hidden * 4,
            transcendentals=0,
        ),
    )(where, layer_one, features)


def blocks_kernel(target, source, count, own, paired, up_a, down_a, up_b, down_b, adjacency, out, held):
    size = adjacency.shape[1]
    strip = own.shape[1]
    out[...] = jnp.zeros_like(out)
    blocks = held.shape[0]
    for b in range(blocks):
        side, at = divmod(b, blocks // 2)
        at = slice(at * size, (at + 1) * size)
        totals = [
            (own[2 * k + side, :, at] + paired[2 * k + side, :, at])
            + (up[side, :, at] + down[side, :, at])
            for k, (up, down) in enumerate(((up_a, down_a), (up_b, down_b)))
        ]
        total = jnp.concatenate(totals, axis=0)
        upper = total.astype(jnp.bfloat16)
        held[b, : 2 * strip] = upper
        held[b, 2 * strip :] = (total - upper.astype(jnp.float32)).astype(jnp.bfloat16)

    def product(s):
        value = lax.dot_general(
            held[source[s]], adjacency[s], NT, preferred_element_type=jnp.float32
        )
        return value[: 2 * strip] + value[2 * strip :]

    group = 16
    live = count[0]
    full = live // group

    def whole(i, before):
        products = [product(i * group + k) for k in range(group)]
        for k in range(group):
            out[target[(i - 1) * group + k]] += before[k]
        return products

    last = lax.fori_loop(1, full, whole, [product(k) for k in range(group)])
    for k in range(group):
        out[target[(full - 1) * group + k]] += last[k]

    def single(s, carry):
        out[target[s]] += product(s)
        return carry

    lax.fori_loop(full * group, live, single, 0)


def blocks(target, source, count, own, paired, streams, adjacency, target_blocks):
    slots, size, _ = adjacency.shape
    parts, strip, half_rows = own.shape
    width = parts // 2 * strip
    return pl.pallas_call(
        blocks_kernel,
        in_specs=[SMEM] * 3 + [VMEM] * 7,
        out_specs=VMEM,
        out_shape=jax.ShapeDtypeStruct((target_blocks, width, size), jnp.float32),
        scratch_shapes=[pltpu.VMEM((2 * half_rows // size, 2 * width, size), jnp.bfloat16)],
        name="blocks",
        compiler_params=pltpu.CompilerParams(vmem_limit_bytes=8 * 2**20),
        cost_estimate=pl.CostEstimate(
            flops=2 * slots * size * size * width,
            bytes_accessed=slots * size * size * 2,
            transcendentals=0,
        ),
    )(target, source, count, own, paired, *streams[0], *streams[1], adjacency)


def second_kernel(where, sums, bias_one, self_weight, neigh_weight, bias_two, seeds, neighbors, out):
    hidden = jnp.maximum(sums[...] + bias_one[...], 0.0).astype(jnp.bfloat16)
    count, fan = neighbors.shape
    positions = lax.broadcasted_iota(jnp.int32, (count, hidden.shape[1]), 1) - where[1] * T_DEV
    pick_self = (positions == seeds[...]).astype(jnp.bfloat16)
    tally = jnp.zeros(positions.shape, jnp.float32)
    for k in range(fan):
        tally += (positions == neighbors[:, k : k + 1]).astype(jnp.float32)
    weights_mean = (tally / fan).astype(jnp.bfloat16)
    self_rows = lax.dot_general(pick_self, hidden, NT, preferred_element_type=jnp.float32)
    neigh_mean = lax.dot_general(weights_mean, hidden, NT, preferred_element_type=jnp.float32)
    out[...] = (
        jnp.dot(
            self_rows.astype(jnp.bfloat16), self_weight[...], preferred_element_type=jnp.float32
        )
        + jnp.dot(
            neigh_mean.astype(jnp.bfloat16), neigh_weight[...], preferred_element_type=jnp.float32
        )
        + bias_two[...]
    )


def second(where, sums, bias_one, self_weight, neigh_weight, bias_two, seeds, neighbors):
    vmem = pl.BlockSpec(memory_space=pltpu.VMEM)
    return pl.pallas_call(
        second_kernel,
        in_specs=[pl.BlockSpec(memory_space=pltpu.SMEM)] + [vmem] * 7,
        out_specs=vmem,
        out_shape=jax.ShapeDtypeStruct((seeds.shape[0], bias_two.shape[0]), jnp.float32),
        name="second",
        compiler_params=pltpu.CompilerParams(vmem_limit_bytes=16 * 2**20),
    )(
        where,
        sums,
        bias_one[:, None],
        self_weight,
        neigh_weight,
        bias_two[None, :],
        seeds[:, None],
        neighbors,
    )


def on_device(
    features,
    adjacency,
    target_block,
    source_block,
    block_count,
    layer_one,
    bias_one,
    self_weight,
    neigh_weight,
    bias_two,
    seed_ids,
    neighbor_ids,
):
    size = adjacency.shape[1]
    node_count = lax.axis_size("node")
    feat_count = lax.axis_size("feat")
    chips = feat_count // 2
    hidden = layer_one.shape[1]
    width = hidden // feat_count
    target_blocks = T_DEV * node_count * feat_count // size
    feat = lax.axis_index("feat")
    where = jnp.stack([feat >> 1, feat & 1]).astype(jnp.int32)

    pair = [(i, i ^ 1) for i in range(feat_count)]
    up = [(i, (i + 2) % feat_count) for i in range(feat_count)]
    down = [((i + 2) % feat_count, i) for i in range(feat_count)]

    def send(value, route):
        return lax.ppermute(value, "feat", route)

    parts = project(where, layer_one, features)
    opposite, three, rest = [send(part, pair) for part in parts[:3]]
    opposite_own, three_own, rest_own = parts[3:]
    strip, half_rows = opposite.shape[1:]

    tie = lax.optimization_barrier
    opposite = (opposite_own + opposite).reshape(2, 2, strip, half_rows)
    zero = jnp.float32(0)
    streams = []
    for k in range(2):
        onward, back, opposite = tie((opposite[k, 0], opposite[k, 1], opposite))
        streams.append((send(onward, up), send(back, down)))
    three = three.reshape(2, 2, 2, strip, half_rows)
    three_own = three_own.reshape(2, 2, 2, strip, half_rows)
    for k, (onward, back) in enumerate(streams):
        onward = lax.pad(onward[None], zero, ((0, 1, 0), (0, 0, 0), (0, 0, 0)))
        back = lax.pad(back[None], zero, ((1, 0, 0), (0, 0, 0), (0, 0, 0)))
        onward, back, three, three_own = tie(
            (
                three_own[0, k] + three[0, k] + onward,
                three_own[1, k] + three[1, k] + back,
                three,
                three_own,
            )
        )
        streams[k] = send(onward, up), send(back, down)
    rest = rest.reshape(5, 2, 2, strip, half_rows)
    rest_own = rest_own.reshape(5, 2, 2, strip, half_rows)
    for hop in (0, 2):
        for k, (onward, back) in enumerate(streams):
            onward, back, rest, rest_own = tie(
                (
                    rest_own[hop, k] + rest[hop, k] + onward,
                    rest_own[hop + 1, k] + rest[hop + 1, k] + back,
                    rest,
                    rest_own,
                )
            )
            streams[k] = send(onward, up), send(back, down)

    partial = blocks(
        target_block,
        source_block,
        block_count,
        rest_own[4].reshape(4, strip, half_rows),
        rest[4].reshape(4, strip, half_rows),
        streams,
        adjacency,
        target_blocks,
    )

    partial = partial.reshape(node_count, chips, width, size)
    summed = jnp.sum(lax.all_to_all(partial, "node", 0, 0), axis=0)
    doubled = jnp.broadcast_to(summed[:, None], (chips, 2, width, size))
    sums = lax.all_to_all(doubled.reshape(feat_count, width, size), "feat", 0, 0)
    return second(
        where,
        sums.reshape(hidden, size),
        bias_one,
        self_weight,
        neigh_weight,
        bias_two,
        seed_ids,
        neighbor_ids,
    )


def solution(mesh):
    placed = (
        P("node", "feat"),
        P("node", None, None),
        P("node"),
        P("node"),
        P("node"),
        P("feat", None),
        P(),
        P(),
        P(),
        P(),
        P(("node", "feat")),
        P(("node", "feat"), None),
    )
    return jax.shard_map(
        on_device, mesh=mesh, in_specs=placed, out_specs=P(("node", "feat"), None), check_vma=False
    )
```

```python
import jax
import jax.numpy as jnp
from jax import lax
from jax.experimental import pallas as pl
from jax.experimental.pallas import tpu as pltpu
from jax.sharding import PartitionSpec as P

T_DEV = 64
NT = (((1,), (1,)), ((), ()))


VMEM = pl.BlockSpec(memory_space=pltpu.VMEM)
SMEM = pl.BlockSpec(memory_space=pltpu.SMEM)


def project_kernel(where, layer_one, features, *refs):
    outs, (held, landed) = refs[:6], refs[6:]
    chips, streams = 8, 2
    strip = outs[0].shape[1]
    tiles, tile = held.shape[:2]
    copies = [
        pltpu.make_async_copy(features.at[pl.ds(i * tile, tile)], held.at[i], landed.at[i])
        for i in range(tiles)
    ]
    for copy in copies:
        copy.start()

    width = streams * strip
    hidden = layer_one.shape[1]
    row = lax.broadcasted_iota(jnp.int32, (hidden, hidden), 0)
    column = lax.broadcasted_iota(jnp.int32, (hidden, hidden), 1)
    half = hidden // 2
    core = (where[1] + (row < half).astype(jnp.int32)) % 2
    place = (row % half) // width
    hop = (place + 1) // 2
    hop = chips // 2 + jnp.where(place % 2 == 1, -hop, hop)
    chip = (where[0] + hop) % chips
    wanted = (chip * 2 + core) * width + row % width
    pick = (column == wanted).astype(jnp.bfloat16)
    ordered = lax.dot_general(
        pick, layer_one[...], NT, preferred_element_type=jnp.float32
    ).astype(jnp.bfloat16)

    for i in range(tiles):
        copies[i].wait()
        product = lax.dot_general(ordered, held[i], NT, preferred_element_type=jnp.float32)
        side, at = divmod(i, tiles // 2)
        take = 0
        for out in outs:
            for k in range(out.shape[0] // 2):
                out[2 * k + side, :, at * tile : (at + 1) * tile] = product[take : take + strip]
                take += strip


def project(where, layer_one, features):
    rows, columns = features.shape
    hidden = layer_one.shape[1]
    strip = hidden // 32
    tiles = 16
    shapes = [
        jax.ShapeDtypeStruct((4 * hops, strip, rows // 2), jnp.float32) for hops in (1, 2, 5)
    ] * 2
    return pl.pallas_call(
        project_kernel,
        in_specs=[SMEM, VMEM, pl.BlockSpec(memory_space=pl.ANY)],
        out_specs=[VMEM] * 6,
        out_shape=shapes,
        scratch_shapes=[
            pltpu.VMEM((tiles, rows // tiles, columns), jnp.bfloat16),
            pltpu.SemaphoreType.DMA((tiles,)),
        ],
        name="project",
        compiler_params=pltpu.CompilerParams(vmem_limit_bytes=44 * 2**20),
        cost_estimate=pl.CostEstimate(
            flops=2 * rows * columns * hidden,
            bytes_accessed=rows * columns * 2 + rows * hidden * 4,
            transcendentals=0,
        ),
    )(where, layer_one, features)


def blocks_kernel(lists, first, own, paired, up, down, adjacency, out, held):
    size = adjacency.shape[1]
    strip = own.shape[1]
    out[...] = jnp.zeros_like(out)
    blocks = held.shape[0]
    for b in range(blocks):
        side, at = divmod(b, blocks // 2)
        at = slice(at * size, (at + 1) * size)
        other = (own[side, :, at] + paired[side, :, at]) + (up[side, :, at] + down[side, :, at])
        total = jnp.concatenate([first[side, :, at], other], axis=0)
        upper = total.astype(jnp.bfloat16)
        held[b, : 2 * strip] = upper
        held[b, 2 * strip :] = (total - upper.astype(jnp.float32)).astype(jnp.bfloat16)

    slots = adjacency.shape[0]

    def product(s):
        value = lax.dot_general(
            held[lists[1 + slots + s]], adjacency[s], NT, preferred_element_type=jnp.float32
        )
        return value[: 2 * strip] + value[2 * strip :]

    group = 16
    live = lists[0]
    full = live // group

    def whole(i, before):
        products = [product(i * group + k) for k in range(group)]
        for k in range(group):
            out[lists[1 + (i - 1) * group + k]] += before[k]
        return products

    last = lax.fori_loop(1, full, whole, [product(k) for k in range(group)])
    for k in range(group):
        out[lists[1 + (full - 1) * group + k]] += last[k]

    def single(s, carry):
        out[lists[1 + s]] += product(s)
        return carry

    lax.fori_loop(full * group, live, single, 0)


def blocks(lists, first, own, paired, up, down, adjacency, target_blocks):
    slots, size, _ = adjacency.shape
    _, strip, half_rows = own.shape
    width = 2 * strip
    return pl.pallas_call(
        blocks_kernel,
        in_specs=[SMEM] + [VMEM] * 6,
        out_specs=VMEM,
        out_shape=jax.ShapeDtypeStruct((target_blocks, width, size), jnp.float32),
        scratch_shapes=[pltpu.VMEM((2 * half_rows // size, 2 * width, size), jnp.bfloat16)],
        name="blocks",
        compiler_params=pltpu.CompilerParams(vmem_limit_bytes=8 * 2**20),
        cost_estimate=pl.CostEstimate(
            flops=2 * slots * size * size * width,
            bytes_accessed=slots * size * size * 2,
            transcendentals=0,
        ),
    )(lists, first, own, paired, up, down, adjacency)


def second_kernel(where, sums, bias_one, self_weight, neigh_weight, bias_two, seeds, neighbors, out):
    hidden = jnp.maximum(sums[...] + bias_one[...], 0.0).astype(jnp.bfloat16)
    count, fan = neighbors.shape
    positions = lax.broadcasted_iota(jnp.int32, (count, hidden.shape[1]), 1) - where[1] * T_DEV
    pick_self = (positions == seeds[...]).astype(jnp.bfloat16)
    tally = jnp.zeros(positions.shape, jnp.float32)
    for k in range(fan):
        tally += (positions == neighbors[:, k : k + 1]).astype(jnp.float32)
    weights_mean = (tally / fan).astype(jnp.bfloat16)
    self_rows = lax.dot_general(pick_self, hidden, NT, preferred_element_type=jnp.float32)
    neigh_mean = lax.dot_general(weights_mean, hidden, NT, preferred_element_type=jnp.float32)
    out[...] = (
        jnp.dot(
            self_rows.astype(jnp.bfloat16), self_weight[...], preferred_element_type=jnp.float32
        )
        + jnp.dot(
            neigh_mean.astype(jnp.bfloat16), neigh_weight[...], preferred_element_type=jnp.float32
        )
        + bias_two[...]
    )


def second(where, sums, bias_one, self_weight, neigh_weight, bias_two, seeds, neighbors):
    vmem = pl.BlockSpec(memory_space=pltpu.VMEM)
    return pl.pallas_call(
        second_kernel,
        in_specs=[pl.BlockSpec(memory_space=pltpu.SMEM)] + [vmem] * 7,
        out_specs=vmem,
        out_shape=jax.ShapeDtypeStruct((seeds.shape[0], bias_two.shape[0]), jnp.float32),
        name="second",
        compiler_params=pltpu.CompilerParams(vmem_limit_bytes=16 * 2**20),
    )(
        where,
        sums,
        bias_one[:, None],
        self_weight,
        neigh_weight,
        bias_two[None, :],
        seeds[:, None],
        neighbors,
    )


def on_device(
    features,
    adjacency,
    target_block,
    source_block,
    block_count,
    layer_one,
    bias_one,
    self_weight,
    neigh_weight,
    bias_two,
    seed_ids,
    neighbor_ids,
):
    size = adjacency.shape[1]
    node_count = lax.axis_size("node")
    feat_count = lax.axis_size("feat")
    chips = feat_count // 2
    hidden = layer_one.shape[1]
    width = hidden // feat_count
    target_blocks = T_DEV * node_count * feat_count // size
    feat = lax.axis_index("feat")
    where = jnp.stack([feat >> 1, feat & 1]).astype(jnp.int32)

    pair = [(i, i ^ 1) for i in range(feat_count)]
    up = [(i, (i + 2) % feat_count) for i in range(feat_count)]
    down = [((i + 2) % feat_count, i) for i in range(feat_count)]

    def send(value, route):
        return lax.ppermute(value, "feat", route)

    parts = project(where, layer_one, features)
    tie = lax.optimization_barrier
    opposite, *others = tie((send(parts[0], pair), *parts[1:3]))
    opposite_own = parts[3]
    strip, half_rows = opposite.shape[1:]

    zero = jnp.float32(0)
    opposite = (opposite_own + opposite).reshape(2, 2, strip, half_rows)
    three, rest = [send(part, pair).reshape(-1, 2, 2, strip, half_rows) for part in others]
    three_own, rest_own = [part.reshape(-1, 2, 2, strip, half_rows) for part in parts[4:]]
    lists = jnp.concatenate([block_count, target_block, source_block])

    streams = [None, None]
    for step in range(5):
        for k in range(2):
            turn = step - k
            if not 0 <= turn <= 3:
                continue
            if turn == 0:
                opposite, lists = tie((opposite, lists))
                onward, back = opposite[k, 0], opposite[k, 1]
            else:
                onward, back = streams[k]
                if turn == 1:
                    three, three_own, lists = tie((three, three_own, lists))
                    onward = lax.pad(onward[None], zero, ((0, 1, 0), (0, 0, 0), (0, 0, 0)))
                    back = lax.pad(back[None], zero, ((1, 0, 0), (0, 0, 0), (0, 0, 0)))
                    onward = three_own[0, k] + three[0, k] + onward
                    back = three_own[1, k] + three[1, k] + back
                else:
                    if step == 4:
                        rest, rest_own, *streams[0] = tie((rest, rest_own, *streams[0]))
                    rest, rest_own, lists = tie((rest, rest_own, lists))
                    at = 2 * turn - 4
                    onward = rest_own[at, k] + rest[at, k] + onward
                    back = rest_own[at + 1, k] + rest[at + 1, k] + back
            onward, back, lists = tie((onward, back, lists))
            streams[k] = send(onward, up), send(back, down)

    onward, back = streams[0]
    first = rest_own[4, 0] + rest[4, 0] + onward + back
    partial = blocks(
        lists, first, rest_own[4, 1], rest[4, 1], *streams[1], adjacency, target_blocks
    )

    partial = partial.reshape(node_count, chips, width, size)
    summed = jnp.sum(lax.all_to_all(partial, "node", 0, 0), axis=0)
    doubled = jnp.broadcast_to(summed[:, None], (chips, 2, width, size))
    sums = lax.all_to_all(doubled.reshape(feat_count, width, size), "feat", 0, 0)
    return second(
        where,
        sums.reshape(hidden, size),
        bias_one,
        self_weight,
        neigh_weight,
        bias_two,
        seed_ids,
        neighbor_ids,
    )


def solution(mesh):
    placed = (
        P("node", "feat"),
        P("node", None, None),
        P("node"),
        P("node"),
        P("node"),
        P("feat", None),
        P(),
        P(),
        P(),
        P(),
        P(("node", "feat")),
        P(("node", "feat"), None),
    )
    return jax.shard_map(
        on_device, mesh=mesh, in_specs=placed, out_specs=P(("node", "feat"), None), check_vma=False
    )
```

```python
import jax
import jax.numpy as jnp
from jax import lax
from jax.experimental import pallas as pl
from jax.experimental.pallas import tpu as pltpu
from jax.sharding import PartitionSpec as P

T_DEV = 64
CHIPS = 8
TILE = 8
RUNS = 8
SPANS = ((0, 10), (10, 16))
NT = (((1,), (1,)), ((), ()))
VMEM = pl.BlockSpec(memory_space=pltpu.VMEM)

UNITS = 2 * RUNS


def project_kernel(ordered, features, *outs):
    lanes = outs[0].shape[2]
    tile = min(512, lanes)
    for i in range(features.shape[0] // tile):
        rows = features[i * tile : (i + 1) * tile]
        product = lax.dot_general(ordered[...], rows, NT, preferred_element_type=jnp.float32)
        run, at = divmod(i * tile, lanes)
        take = 0
        for out in outs:
            for k in range(out.shape[0] // RUNS):
                out[k * RUNS + run, :, at : at + tile] = product[take : take + TILE]
                take += TILE


def project(ordered, features):
    rows, columns = features.shape
    hidden = ordered.shape[0]
    shapes = [
        jax.ShapeDtypeStruct((strips * UNITS, TILE, rows // RUNS), jnp.float32)
        for strips in (1, CHIPS - 1)
    ] * 2
    return pl.pallas_call(
        project_kernel,
        in_specs=[VMEM] * 2,
        out_specs=[VMEM] * 4,
        out_shape=shapes,
        name="project",
        compiler_params=pltpu.CompilerParams(vmem_limit_bytes=8 * 2**20),
        cost_estimate=pl.CostEstimate(
            flops=2 * rows * columns * hidden,
            bytes_accessed=rows * columns * 2 + rows * hidden * 4,
            transcendentals=0,
        ),
    )(ordered, features)


def in_hop_order(layer_one):
    hidden = layer_one.shape[1]
    feat = lax.axis_index("feat")
    row = jnp.arange(hidden, dtype=jnp.int32)
    place = row % (hidden // 2) // (2 * TILE)
    hop = (place + 1) // 2
    hop = CHIPS // 2 + jnp.where(place % 2 == 1, -hop, hop)
    chip = ((feat >> 1) + hop) % CHIPS
    core = ((feat & 1) + (row < hidden // 2)) % 2
    wanted = (chip * 2 + core) * (2 * TILE) + row % (2 * TILE)
    pick = (jnp.arange(hidden, dtype=jnp.int32)[None, :] == wanted[:, None]).astype(jnp.bfloat16)
    return lax.dot_general(pick, layer_one, NT, preferred_element_type=jnp.float32).astype(
        jnp.bfloat16
    )


def blocks_kernel(
    lists, own, paired, up_a, down_a, up_b, down_b, adjacency, out, held, table, landed
):
    copy = pltpu.make_async_copy(lists, table, landed)
    copy.start()
    slots, size, _ = adjacency.shape
    lanes = own.shape[2]
    out[...] = jnp.zeros_like(out)
    for b in range(held.shape[0]):
        run, at = divmod(b * size, lanes)
        at = slice(at, at + size)
        totals = []
        for unit in (run, RUNS + run):
            ups, downs, begin = (up_a, down_a, 0) if unit < SPANS[0][1] else (up_b, down_b, SPANS[1][0])
            totals.append(
                (own[unit, :, at] + paired[unit, :, at])
                + (ups[unit - begin, :, at] + downs[unit - begin, :, at])
            )
        total = jnp.concatenate(totals, axis=0)
        upper = total.astype(jnp.bfloat16)
        held[b, : 2 * TILE] = upper
        held[b, 2 * TILE :] = (total - upper.astype(jnp.float32)).astype(jnp.bfloat16)
    copy.wait()

    def product(s):
        value = lax.dot_general(
            held[table[slots + s]], adjacency[s], NT, preferred_element_type=jnp.float32
        )
        return value[: 2 * TILE] + value[2 * TILE :]

    def add(s, value):
        block = table[s]
        place = 2 * block - block % CHIPS
        out[place] += value[:TILE]
        out[place + CHIPS] += value[TILE:]

    group = 16
    live = table[2 * slots]
    full = live // group

    def whole(i, before):
        products = [product(i * group + k) for k in range(group)]
        for k in range(group):
            add((i - 1) * group + k, before[k])
        return products

    last = lax.fori_loop(1, full, whole, [product(k) for k in range(group)])
    for k in range(group):
        add((full - 1) * group + k, last[k])

    def single(s, carry):
        add(s, product(s))
        return carry

    lax.fori_loop(full * group, live, single, 0)


def blocks(lists, own, paired, streams, adjacency, target_blocks):
    slots, size, _ = adjacency.shape
    rows = RUNS * own.shape[2]
    return pl.pallas_call(
        blocks_kernel,
        in_specs=[pl.BlockSpec(memory_space=pl.ANY)] + [VMEM] * 7,
        out_specs=VMEM,
        out_shape=jax.ShapeDtypeStruct((2 * target_blocks, TILE, size), jnp.float32),
        scratch_shapes=[
            pltpu.VMEM((rows // size, 4 * TILE, size), jnp.bfloat16),
            pltpu.SMEM(lists.shape, jnp.int32),
            pltpu.SemaphoreType.DMA,
        ],
        name="blocks",
        compiler_params=pltpu.CompilerParams(vmem_limit_bytes=8 * 2**20),
        cost_estimate=pl.CostEstimate(
            flops=4 * slots * size * size * UNITS,
            bytes_accessed=slots * size * size * 2,
            transcendentals=0,
        ),
    )(lists, own, paired, *streams[0], *streams[1], adjacency)


def combine_kernel(parts, out):
    size = parts.shape[3]
    low = lax.broadcasted_iota(jnp.int32, (TILE, size), 1) < T_DEV
    for chip in range(CHIPS):
        left, right = parts[0, chip], parts[0, CHIPS + chip]
        for n in range(1, parts.shape[0]):
            left += parts[n, chip]
            right += parts[n, CHIPS + chip]
        out[2 * chip] = jnp.where(low, left, pltpu.roll(right, T_DEV, 1))
        out[2 * chip + 1] = jnp.where(low, pltpu.roll(left, T_DEV, 1), right)


def combine(parts):
    return pl.pallas_call(
        combine_kernel,
        in_specs=[VMEM],
        out_specs=VMEM,
        out_shape=jax.ShapeDtypeStruct(parts.shape[1:], jnp.float32),
        name="combine",
        compiler_params=pltpu.CompilerParams(vmem_limit_bytes=4 * 2**20),
    )(parts)


def second_kernel(parts, bias_one, self_weight, neigh_weight, bias_two, seeds, neighbors, out):
    rows = []
    for k in range(parts.shape[0]):
        rows += [parts[k], pltpu.roll(parts[k], T_DEV, 1)]
    sums = jnp.concatenate(rows, axis=0)
    hidden = jnp.maximum(sums + bias_one[...], 0.0).astype(jnp.bfloat16)
    count, fan = neighbors.shape
    positions = lax.broadcasted_iota(jnp.int32, (count, hidden.shape[1]), 1)
    pick_self = (positions == seeds[...]).astype(jnp.float32)
    tally = jnp.zeros(positions.shape, jnp.float32)
    for k in range(fan):
        tally += (positions == neighbors[:, k : k + 1]).astype(jnp.float32)
    picked = lax.dot_general(
        jnp.concatenate([pick_self, tally / fan], axis=0).astype(jnp.bfloat16),
        hidden,
        NT,
        preferred_element_type=jnp.float32,
    ).astype(jnp.bfloat16)
    out[...] = (
        lax.dot_general(
            picked[:count], self_weight[...], NT, preferred_element_type=jnp.float32
        )
        + lax.dot_general(
            picked[count:], neigh_weight[...], NT, preferred_element_type=jnp.float32
        )
        + bias_two[...]
    )


def second(parts, bias_one, self_weight, neigh_weight, bias_two, seeds, neighbors):
    return pl.pallas_call(
        second_kernel,
        in_specs=[VMEM] * 7,
        out_specs=VMEM,
        out_shape=jax.ShapeDtypeStruct((seeds.shape[0], bias_two.shape[0]), jnp.float32),
        name="second",
        compiler_params=pltpu.CompilerParams(vmem_limit_bytes=8 * 2**20),
    )(
        parts,
        bias_one[:, None],
        self_weight.T,
        neigh_weight.T,
        bias_two[None, :],
        seeds[:, None],
        neighbors,
    )


def on_device(
    features,
    adjacency,
    target_block,
    source_block,
    block_count,
    layer_one,
    bias_one,
    self_weight,
    neigh_weight,
    bias_two,
    seed_ids,
    neighbor_ids,
):
    size = adjacency.shape[1]
    node_count = lax.axis_size("node")
    feat_count = lax.axis_size("feat")
    target_blocks = T_DEV * node_count * feat_count // size

    pair = [(i, i ^ 1) for i in range(feat_count)]
    up = [(i, (i + 2) % feat_count) for i in range(feat_count)]
    down = [((i + 2) % feat_count, i) for i in range(feat_count)]

    def send(value, route):
        return lax.ppermute(value, "feat", route)

    tie = lax.optimization_barrier
    opposite, rest, opposite_own, rest_own = project(in_hop_order(layer_one), features)
    opposite, rest = tie((send(opposite, pair), rest))
    rest = send(rest, pair)

    order = block_count
    streams = []
    for begin, end in SPANS:
        middle = (end - begin) // 2
        opposite, opposite_own, order = tie((opposite, opposite_own, order))
        onward = opposite_own[begin : begin + middle] + opposite[begin : begin + middle]
        back = opposite_own[begin + middle : end] + opposite[begin + middle : end]
        onward, back, order = tie((onward, back, order))
        streams.append((send(onward, up), send(back, down)))
    for turn in range(3):
        for k, (begin, end) in enumerate(SPANS):
            onward, back = streams[k]
            if turn == 0:
                zero = jnp.float32(0)
                onward = lax.pad(onward, zero, ((0, (end - begin) // 2, 0), (0, 0, 0), (0, 0, 0)))
                back = lax.pad(back, zero, (((end - begin) // 2, 0, 0), (0, 0, 0), (0, 0, 0)))
            rest, rest_own, order = tie((rest, rest_own, order))
            at = 2 * turn * UNITS
            onward = rest_own[at + begin : at + end] + rest[at + begin : at + end] + onward
            at += UNITS
            back = rest_own[at + begin : at + end] + rest[at + begin : at + end] + back
            onward, back, order = tie((onward, back, order))
            streams[k] = send(onward, up), send(back, down)

    lists = jnp.concatenate([target_block, source_block, block_count])
    partial = blocks(
        lists, rest_own[6 * UNITS :], rest[6 * UNITS :], streams, adjacency, target_blocks
    )

    partial = partial.reshape(node_count, 2 * CHIPS, TILE, size)
    parts = combine(lax.all_to_all(partial, "node", 0, 0))
    parts = lax.all_to_all(parts, "feat", 0, 0)
    return second(
        parts, bias_one, self_weight, neigh_weight, bias_two, seed_ids, neighbor_ids
    )


def solution(mesh):
    placed = (
        P("node", "feat"),
        P("node", None, None),
        P("node"),
        P("node"),
        P("node"),
        P("feat", None),
        P(),
        P(),
        P(),
        P(),
        P(("node", "feat")),
        P(("node", "feat"), None),
    )
    return jax.shard_map(
        on_device, mesh=mesh, in_specs=placed, out_specs=P(("node", "feat"), None), check_vma=False
    )
```

```python
import jax
import jax.numpy as jnp
from jax import lax
from jax.experimental import pallas as pl
from jax.experimental.pallas import tpu as pltpu
from jax.sharding import PartitionSpec as P

T_DEV = 64
CHIPS = 8
TILE = 8
RUNS = 8
SPANS = ((0, 10), (10, 16))
GROUP = 16
NT = (((1,), (1,)), ((), ()))
VMEM = pl.BlockSpec(memory_space=pltpu.VMEM)

UNITS = 2 * RUNS


def project_kernel(ordered, features, *outs):
    lanes = outs[0].shape[2]
    tile = min(512, lanes)
    for i in range(features.shape[0] // tile):
        rows = features[i * tile : (i + 1) * tile]
        product = lax.dot_general(ordered[...], rows, NT, preferred_element_type=jnp.float32)
        run, at = divmod(i * tile, lanes)
        take = 0
        for out in outs:
            for k in range(out.shape[0] // RUNS):
                unit = k // 2 * UNITS + 2 * run + k % 2
                out[unit, :, at : at + tile] = product[take : take + TILE]
                take += TILE


def project(ordered, features):
    rows, columns = features.shape
    hidden = ordered.shape[0]
    shapes = [
        jax.ShapeDtypeStruct((strips * UNITS, TILE, rows // RUNS), jnp.float32)
        for strips in (1, CHIPS - 1)
    ] * 2
    return pl.pallas_call(
        project_kernel,
        in_specs=[VMEM] * 2,
        out_specs=[VMEM] * 4,
        out_shape=shapes,
        name="project",
        compiler_params=pltpu.CompilerParams(vmem_limit_bytes=8 * 2**20),
        cost_estimate=pl.CostEstimate(
            flops=2 * rows * columns * hidden,
            bytes_accessed=rows * columns * 2 + rows * hidden * 4,
            transcendentals=0,
        ),
    )(ordered, features)


def in_hop_order(layer_one):
    hidden = layer_one.shape[1]
    feat = lax.axis_index("feat")
    row = jnp.arange(hidden, dtype=jnp.int32)
    place = row % (hidden // 2) // (2 * TILE)
    hop = (place + 1) // 2
    hop = CHIPS // 2 + jnp.where(place % 2 == 1, -hop, hop)
    chip = ((feat >> 1) + hop) % CHIPS
    core = ((feat & 1) + (row < hidden // 2)) % 2
    wanted = (chip * 2 + core) * (2 * TILE) + row % (2 * TILE)
    pick = (jnp.arange(hidden, dtype=jnp.int32)[None, :] == wanted[:, None]).astype(jnp.bfloat16)
    return lax.dot_general(pick, layer_one, NT, preferred_element_type=jnp.float32).astype(
        jnp.bfloat16
    )


def block_lists(target_block, source_block, block_count, early):
    place = 2 * target_block - target_block % CHIPS
    slots = target_block.shape[0]
    slot = jnp.arange(slots, dtype=jnp.int32)
    live = slot < block_count[0]
    key = jnp.where(live, (source_block >= early).astype(jnp.int32), 2)
    key = key * slots + slot
    rank = jnp.sum((key[None, :] < key[:, None]).astype(jnp.int32), axis=1)
    at = rank[None, :] == slot[:, None]
    lists = [
        jnp.sum(jnp.where(at, values[None, :], 0), axis=1)
        for values in (place, source_block, slot)
    ]
    first = jnp.sum((key < slots).astype(jnp.int32))[None]
    spare = jnp.zeros((GROUP,), jnp.int32)
    pieces = [piece for values in lists for piece in (values, spare)]
    return jnp.concatenate([*pieces, first, block_count])


def block_products(late, lists, own, paired, up, down, adjacency, out, held, table, landed):
    copy = pltpu.make_async_copy(lists, table, landed)
    copy.start()
    slots, size, _ = adjacency.shape
    lanes = own.shape[2]
    begin = SPANS[late][0]
    for b in range(begin // 2 * lanes // size, SPANS[late][1] // 2 * lanes // size):
        run, at = divmod(b * size, lanes)
        at = slice(at, at + size)
        total = jnp.concatenate(
            [
                (own[unit, :, at] + paired[unit, :, at])
                + (up[unit - begin, :, at] + down[unit - begin, :, at])
                for unit in (2 * run, 2 * run + 1)
            ],
            axis=0,
        )
        upper = total.astype(jnp.bfloat16)
        held[b, : 2 * TILE] = upper
        held[b, 2 * TILE :] = (total - upper.astype(jnp.float32)).astype(jnp.bfloat16)
    copy.wait()
    step = slots + GROUP
    counts = table[3 * step], table[3 * step + 1]
    start = counts[0] if late else 0
    end = counts[late]

    def products(first):
        values = []
        for k in range(0, GROUP, 2):
            left = [held[table[step + first + k + j]] for j in range(2)]
            right = [adjacency[table[2 * step + first + k + j]] for j in range(2)]
            value = lax.dot_general(
                jnp.concatenate(left, axis=0),
                jnp.concatenate(right, axis=0),
                NT,
                preferred_element_type=jnp.float32,
            )
            rows = 2 * TILE
            values.append(value[:rows, :size] + value[rows : 2 * rows, :size])
            values.append(value[2 * rows : 3 * rows, size:] + value[3 * rows :, size:])
        return values

    def add(first, values):
        for k in range(GROUP):
            place = table[first + k]
            value = jnp.where(first + k < end, values[k], 0.0)
            out[place] += value[:TILE]
            out[place + CHIPS] += value[TILE:]

    def whole(i, before):
        after = products(start + i * GROUP)
        add(start + (i - 1) * GROUP, before)
        return after

    groups = (end - start + GROUP - 1) // GROUP
    last = lax.fori_loop(1, groups, whole, products(start))
    add(start + (jnp.maximum(groups, 1) - 1) * GROUP, last)


def early_kernel(lists, own, paired, up, down, adjacency, out, held, table, landed):
    out[...] = jnp.zeros_like(out)
    block_products(0, lists, own, paired, up, down, adjacency, out, held, table, landed)


def late_kernel(before, lists, own, paired, up, down, adjacency, out, held, table, landed):
    out[...] = before[...]
    block_products(1, lists, own, paired, up, down, adjacency, out, held, table, landed)


def blocks(before, lists, own, paired, stream, adjacency, target_blocks):
    slots, size, _ = adjacency.shape
    rows = RUNS * own.shape[2]
    late = before is not None
    return pl.pallas_call(
        late_kernel if late else early_kernel,
        in_specs=[VMEM] * late + [pl.BlockSpec(memory_space=pl.ANY)] + [VMEM] * 5,
        out_specs=VMEM,
        out_shape=jax.ShapeDtypeStruct((2 * target_blocks, TILE, size), jnp.float32),
        scratch_shapes=[
            pltpu.VMEM((rows // size, 4 * TILE, size), jnp.bfloat16),
            pltpu.SMEM(lists.shape, jnp.int32),
            pltpu.SemaphoreType.DMA,
        ],
        name="late_blocks" if late else "early_blocks",
        compiler_params=pltpu.CompilerParams(vmem_limit_bytes=8 * 2**20),
        cost_estimate=pl.CostEstimate(
            flops=4 * slots * size * size * UNITS,
            bytes_accessed=slots * size * size,
            transcendentals=0,
        ),
    )(*([before] if late else []), lists, own, paired, *stream, adjacency)


def combine_kernel(parts, out):
    size = parts.shape[3]
    low = lax.broadcasted_iota(jnp.int32, (TILE, size), 1) < T_DEV
    for chip in range(CHIPS):
        left, right = parts[0, chip], parts[0, CHIPS + chip]
        for n in range(1, parts.shape[0]):
            left += parts[n, chip]
            right += parts[n, CHIPS + chip]
        out[2 * chip] = jnp.where(low, left, pltpu.roll(right, T_DEV, 1))
        out[2 * chip + 1] = jnp.where(low, pltpu.roll(left, T_DEV, 1), right)


def combine(parts):
    return pl.pallas_call(
        combine_kernel,
        in_specs=[VMEM],
        out_specs=VMEM,
        out_shape=jax.ShapeDtypeStruct(parts.shape[1:], jnp.float32),
        name="combine",
        compiler_params=pltpu.CompilerParams(vmem_limit_bytes=4 * 2**20),
    )(parts)


def second_kernel(parts, bias_one, self_weight, neigh_weight, bias_two, seeds, neighbors, out):
    rows = []
    for k in range(parts.shape[0]):
        rows += [parts[k], pltpu.roll(parts[k], T_DEV, 1)]
    sums = jnp.concatenate(rows, axis=0)
    hidden = jnp.maximum(sums + bias_one[...], 0.0).astype(jnp.bfloat16)
    count, fan = neighbors.shape
    positions = lax.broadcasted_iota(jnp.int32, (count, hidden.shape[1]), 1)
    pick_self = (positions == seeds[...]).astype(jnp.float32)
    tally = jnp.zeros(positions.shape, jnp.float32)
    for k in range(fan):
        tally += (positions == neighbors[:, k : k + 1]).astype(jnp.float32)
    picked = lax.dot_general(
        jnp.concatenate([pick_self, tally / fan], axis=0).astype(jnp.bfloat16),
        hidden,
        NT,
        preferred_element_type=jnp.float32,
    ).astype(jnp.bfloat16)
    out[...] = (
        lax.dot_general(
            picked[:count], self_weight[...], NT, preferred_element_type=jnp.float32
        )
        + lax.dot_general(
            picked[count:], neigh_weight[...], NT, preferred_element_type=jnp.float32
        )
        + bias_two[...]
    )


def second(parts, bias_one, self_weight, neigh_weight, bias_two, seeds, neighbors):
    return pl.pallas_call(
        second_kernel,
        in_specs=[VMEM] * 7,
        out_specs=VMEM,
        out_shape=jax.ShapeDtypeStruct((seeds.shape[0], bias_two.shape[0]), jnp.float32),
        name="second",
        compiler_params=pltpu.CompilerParams(vmem_limit_bytes=8 * 2**20),
    )(
        parts,
        bias_one[:, None],
        self_weight.T,
        neigh_weight.T,
        bias_two[None, :],
        seeds[:, None],
        neighbors,
    )


def on_device(
    features,
    adjacency,
    target_block,
    source_block,
    block_count,
    layer_one,
    bias_one,
    self_weight,
    neigh_weight,
    bias_two,
    seed_ids,
    neighbor_ids,
):
    size = adjacency.shape[1]
    node_count = lax.axis_size("node")
    feat_count = lax.axis_size("feat")
    target_blocks = T_DEV * node_count * feat_count // size

    pair = [(i, i ^ 1) for i in range(feat_count)]
    up = [(i, (i + 2) % feat_count) for i in range(feat_count)]
    down = [((i + 2) % feat_count, i) for i in range(feat_count)]

    def send(value, route):
        return lax.ppermute(value, "feat", route)

    tie = lax.optimization_barrier
    opposite, rest, opposite_own, rest_own = project(in_hop_order(layer_one), features)
    opposite, rest = tie((send(opposite, pair), rest))
    rest = send(rest, pair)

    order = block_count
    streams = []
    for begin, end in SPANS:
        middle = (end - begin) // 2
        opposite, opposite_own, order = tie((opposite, opposite_own, order))
        onward = opposite_own[begin : begin + middle] + opposite[begin : begin + middle]
        back = opposite_own[begin + middle : end] + opposite[begin + middle : end]
        onward, back, order = tie((onward, back, order))
        streams.append((send(onward, up), send(back, down)))
    for turn in range(3):
        for k, (begin, end) in enumerate(SPANS):
            onward, back = streams[k]
            if turn == 0:
                zero = jnp.float32(0)
                onward = lax.pad(onward, zero, ((0, (end - begin) // 2, 0), (0, 0, 0), (0, 0, 0)))
                back = lax.pad(back, zero, (((end - begin) // 2, 0, 0), (0, 0, 0), (0, 0, 0)))
            rest, rest_own, order = tie((rest, rest_own, order))
            at = 2 * turn * UNITS
            onward = rest_own[at + begin : at + end] + rest[at + begin : at + end] + onward
            at += UNITS
            back = rest_own[at + begin : at + end] + rest[at + begin : at + end] + back
            onward, back, order = tie((onward, back, order))
            streams[k] = send(onward, up), send(back, down)

    early = SPANS[0][1] // 2 * (features.shape[0] // RUNS) // size
    lists = block_lists(target_block, source_block, block_count, early)
    near = rest_own[6 * UNITS :], rest[6 * UNITS :]
    partial = blocks(None, lists, *near, streams[0], adjacency, target_blocks)
    partial = blocks(partial, lists, *near, streams[1], adjacency, target_blocks)

    partial = partial.reshape(node_count, 2 * CHIPS, TILE, size)
    parts = combine(lax.all_to_all(partial, "node", 0, 0))
    parts = lax.all_to_all(parts, "feat", 0, 0)
    return second(
        parts, bias_one, self_weight, neigh_weight, bias_two, seed_ids, neighbor_ids
    )


def solution(mesh):
    placed = (
        P("node", "feat"),
        P("node", None, None),
        P("node"),
        P("node"),
        P("node"),
        P("feat", None),
        P(),
        P(),
        P(),
        P(),
        P(("node", "feat")),
        P(("node", "feat"), None),
    )
    return jax.shard_map(
        on_device, mesh=mesh, in_specs=placed, out_specs=P(("node", "feat"), None), check_vma=False
    )
```

```python
import jax
import jax.numpy as jnp
from jax import lax
from jax.experimental import pallas as pl
from jax.experimental.pallas import tpu as pltpu
from jax.sharding import PartitionSpec as P

T_DEV = 64
CHIPS = 8
TILE = 8
RUNS = 8
SPANS = ((0, 10), (10, 16))
GROUP = 16
NT = (((1,), (1,)), ((), ()))
VMEM = pl.BlockSpec(memory_space=pltpu.VMEM)

UNITS = 2 * RUNS


def project_kernel(ordered, features, *outs):
    lanes = outs[0].shape[2]
    tile = min(512, lanes)
    for i in range(features.shape[0] // tile):
        rows = features[i * tile : (i + 1) * tile]
        product = lax.dot_general(ordered[...], rows, NT, preferred_element_type=jnp.float32)
        run, at = divmod(i * tile, lanes)
        take = 0
        for out in outs:
            for k in range(out.shape[0] // RUNS):
                unit = k // 2 * UNITS + 2 * run + k % 2
                out[unit, :, at : at + tile] = product[take : take + TILE]
                take += TILE


def project(ordered, features):
    rows, columns = features.shape
    hidden = ordered.shape[0]
    shapes = [
        jax.ShapeDtypeStruct((strips * UNITS, TILE, rows // RUNS), jnp.float32)
        for strips in (1, CHIPS - 2, 1)
    ] * 2
    return pl.pallas_call(
        project_kernel,
        in_specs=[VMEM] * 2,
        out_specs=[VMEM] * 6,
        out_shape=shapes,
        name="project",
        compiler_params=pltpu.CompilerParams(vmem_limit_bytes=8 * 2**20),
        cost_estimate=pl.CostEstimate(
            flops=2 * rows * columns * hidden,
            bytes_accessed=rows * columns * 2 + rows * hidden * 4,
            transcendentals=0,
        ),
    )(ordered, features)


def in_hop_order(layer_one):
    hidden = layer_one.shape[1]
    feat = lax.axis_index("feat")
    row = jnp.arange(hidden, dtype=jnp.int32)
    place = row % (hidden // 2) // (2 * TILE)
    hop = (place + 1) // 2
    hop = CHIPS // 2 + jnp.where(place % 2 == 1, -hop, hop)
    chip = ((feat >> 1) + hop) % CHIPS
    core = ((feat & 1) + (row < hidden // 2)) % 2
    wanted = (chip * 2 + core) * (2 * TILE) + row % (2 * TILE)
    pick = (jnp.arange(hidden, dtype=jnp.int32)[None, :] == wanted[:, None]).astype(jnp.bfloat16)
    return lax.dot_general(pick, layer_one, NT, preferred_element_type=jnp.float32).astype(
        jnp.bfloat16
    )


def block_lists(target_block, source_block, block_count, early):
    place = 2 * target_block - target_block % CHIPS
    slots = target_block.shape[0]
    slot = jnp.arange(slots, dtype=jnp.int32)
    live = slot < block_count[0]
    key = jnp.where(live, (source_block >= early).astype(jnp.int32), 2)
    key = key * slots + slot
    rank = jnp.sum((key[None, :] < key[:, None]).astype(jnp.int32), axis=1)
    at = rank[None, :] == slot[:, None]
    lists = [
        jnp.sum(jnp.where(at, values[None, :], 0), axis=1)
        for values in (place, source_block, slot)
    ]
    first = jnp.sum((key < slots).astype(jnp.int32))[None]
    spare = jnp.zeros((GROUP,), jnp.int32)
    pieces = [piece for values in lists for piece in (values, spare)]
    return jnp.concatenate([*pieces, first, block_count])


def block_products(late, own, paired, up, down, adjacency, out, held, table, start, end, loaded):
    size = adjacency.shape[1]
    lanes = own.shape[2]
    begin = SPANS[late][0]
    for b in range(begin // 2 * lanes // size, SPANS[late][1] // 2 * lanes // size):
        run, at = divmod(b * size, lanes)
        at = slice(at, at + size)
        total = jnp.concatenate(
            [
                (own[unit, :, at] + paired[unit, :, at])
                + (up[unit - begin, :, at] + down[unit - begin, :, at])
                for unit in (2 * run, 2 * run + 1)
            ],
            axis=0,
        )
        upper = total.astype(jnp.bfloat16)
        held[b, : 2 * TILE] = upper
        held[b, 2 * TILE :] = (total - upper.astype(jnp.float32)).astype(jnp.bfloat16)
    loaded()
    start, end = start(), end()
    step = (table.shape[0] - 2) // 3

    def products(first):
        values = []
        for k in range(0, GROUP, 2):
            left = [held[table[step + first + k + j]] for j in range(2)]
            right = [
                adjacency[first - start + k + j if late else table[2 * step + first + k + j]]
                for j in range(2)
            ]
            value = lax.dot_general(
                jnp.concatenate(left, axis=0),
                jnp.concatenate(right, axis=0),
                NT,
                preferred_element_type=jnp.float32,
            )
            rows = 2 * TILE
            values.append(value[:rows, :size] + value[rows : 2 * rows, :size])
            values.append(value[2 * rows : 3 * rows, size:] + value[3 * rows :, size:])
        return values

    def add(first, values):
        for k in range(GROUP):
            place = table[first + k]
            value = jnp.where(first + k < end, values[k], 0.0)
            out[place] += value[:TILE]
            out[place + CHIPS] += value[TILE:]

    def whole(i, before):
        after = products(start + i * GROUP)
        add(start + (i - 1) * GROUP, before)
        return after

    groups = (end - start + GROUP - 1) // GROUP
    last = lax.fori_loop(1, groups, whole, products(start))
    add(start + (jnp.maximum(groups, 1) - 1) * GROUP, last)


def early_kernel(lists, own, paired, up, down, adjacency, out, kept, held, table, landed):
    copy = pltpu.make_async_copy(lists, table, landed)
    copy.start()
    out[...] = jnp.zeros_like(out)
    step = (table.shape[0] - 2) // 3
    block_products(
        0, own, paired, up, down, adjacency, out, held, table,
        lambda: 0, lambda: table[3 * step], copy.wait,
    )

    def keep(i, carry):
        kept[i - table[3 * step]] = adjacency[table[2 * step + i]]
        return carry

    lax.fori_loop(table[3 * step], table[3 * step + 1], keep, 0)


def late_kernel(before, lists, own, paired, up, down, kept, out, held, table, landed):
    copy = pltpu.make_async_copy(lists, table, landed)
    copy.start()
    out[...] = before[...]
    step = (table.shape[0] - 2) // 3
    block_products(
        1, own, paired, up, down, kept, out, held, table,
        lambda: table[3 * step], lambda: table[3 * step + 1], copy.wait,
    )


def scratch_for(lists, own, size):
    return [
        pltpu.VMEM((RUNS * own.shape[2] // size, 4 * TILE, size), jnp.bfloat16),
        pltpu.SMEM(lists.shape, jnp.int32),
        pltpu.SemaphoreType.DMA,
    ]


def early_blocks(lists, own, paired, stream, adjacency, target_blocks):
    slots, size, _ = adjacency.shape
    return pl.pallas_call(
        early_kernel,
        in_specs=[pl.BlockSpec(memory_space=pl.ANY)] + [VMEM] * 5,
        out_specs=[VMEM] * 2,
        out_shape=[
            jax.ShapeDtypeStruct((2 * target_blocks, TILE, size), jnp.float32),
            jax.ShapeDtypeStruct((slots + GROUP, size, size), adjacency.dtype),
        ],
        scratch_shapes=scratch_for(lists, own, size),
        name="early_blocks",
        compiler_params=pltpu.CompilerParams(vmem_limit_bytes=8 * 2**20),
        cost_estimate=pl.CostEstimate(
            flops=4 * slots * size * size * UNITS,
            bytes_accessed=slots * size * size,
            transcendentals=0,
        ),
    )(lists, own, paired, *stream, adjacency)


def late_blocks(before, lists, own, paired, stream, kept):
    slots, size, _ = kept.shape
    return pl.pallas_call(
        late_kernel,
        in_specs=[VMEM, pl.BlockSpec(memory_space=pl.ANY)] + [VMEM] * 5,
        out_specs=VMEM,
        out_shape=jax.ShapeDtypeStruct(before.shape, jnp.float32),
        scratch_shapes=scratch_for(lists, own, size),
        name="late_blocks",
        compiler_params=pltpu.CompilerParams(vmem_limit_bytes=8 * 2**20),
        cost_estimate=pl.CostEstimate(
            flops=4 * slots * size * size * UNITS,
            bytes_accessed=slots * size * size,
            transcendentals=0,
        ),
    )(before, lists, own, paired, *stream, kept)


def combine_kernel(parts, out):
    size = parts.shape[3]
    low = lax.broadcasted_iota(jnp.int32, (TILE, size), 1) < T_DEV
    for chip in range(CHIPS):
        left, right = parts[0, chip], parts[0, CHIPS + chip]
        for n in range(1, parts.shape[0]):
            left += parts[n, chip]
            right += parts[n, CHIPS + chip]
        out[2 * chip] = jnp.where(low, left, pltpu.roll(right, T_DEV, 1))
        out[2 * chip + 1] = jnp.where(low, pltpu.roll(left, T_DEV, 1), right)


def combine(parts):
    return pl.pallas_call(
        combine_kernel,
        in_specs=[VMEM],
        out_specs=VMEM,
        out_shape=jax.ShapeDtypeStruct(parts.shape[1:], jnp.float32),
        name="combine",
        compiler_params=pltpu.CompilerParams(vmem_limit_bytes=4 * 2**20),
    )(parts)


def second_kernel(parts, bias_one, self_weight, neigh_weight, bias_two, seeds, neighbors, out):
    rows = []
    for k in range(parts.shape[0]):
        rows += [parts[k], pltpu.roll(parts[k], T_DEV, 1)]
    sums = jnp.concatenate(rows, axis=0)
    hidden = jnp.maximum(sums + bias_one[...], 0.0).astype(jnp.bfloat16)
    count, fan = neighbors.shape
    positions = lax.broadcasted_iota(jnp.int32, (count, hidden.shape[1]), 1)
    pick_self = (positions == seeds[...]).astype(jnp.float32)
    tally = jnp.zeros(positions.shape, jnp.float32)
    for k in range(fan):
        tally += (positions == neighbors[:, k : k + 1]).astype(jnp.float32)
    picked = lax.dot_general(
        jnp.concatenate([pick_self, tally / fan], axis=0).astype(jnp.bfloat16),
        hidden,
        NT,
        preferred_element_type=jnp.float32,
    ).astype(jnp.bfloat16)
    out[...] = (
        lax.dot_general(
            picked[:count], self_weight[...], NT, preferred_element_type=jnp.float32
        )
        + lax.dot_general(
            picked[count:], neigh_weight[...], NT, preferred_element_type=jnp.float32
        )
        + bias_two[...]
    )


def second(parts, bias_one, self_weight, neigh_weight, bias_two, seeds, neighbors):
    return pl.pallas_call(
        second_kernel,
        in_specs=[VMEM] * 7,
        out_specs=VMEM,
        out_shape=jax.ShapeDtypeStruct((seeds.shape[0], bias_two.shape[0]), jnp.float32),
        name="second",
        compiler_params=pltpu.CompilerParams(vmem_limit_bytes=8 * 2**20),
    )(
        parts,
        bias_one[:, None],
        self_weight.T,
        neigh_weight.T,
        bias_two[None, :],
        seeds[:, None],
        neighbors,
    )


def on_device(
    features,
    adjacency,
    target_block,
    source_block,
    block_count,
    layer_one,
    bias_one,
    self_weight,
    neigh_weight,
    bias_two,
    seed_ids,
    neighbor_ids,
):
    size = adjacency.shape[1]
    node_count = lax.axis_size("node")
    feat_count = lax.axis_size("feat")
    target_blocks = T_DEV * node_count * feat_count // size

    pair = [(i, i ^ 1) for i in range(feat_count)]
    up = [(i, (i + 2) % feat_count) for i in range(feat_count)]
    down = [((i + 2) % feat_count, i) for i in range(feat_count)]

    def send(value, route):
        return lax.ppermute(value, "feat", route)

    tie = lax.optimization_barrier
    opposite, rest, near, opposite_own, rest_own, near_own = project(
        in_hop_order(layer_one), features
    )
    opposite, rest = tie((send(opposite, pair), rest))
    rest, near = tie((send(rest, pair), near))
    near = send(near, pair)

    order = block_count
    streams = []
    for begin, end in SPANS:
        middle = (end - begin) // 2
        opposite, opposite_own, order = tie((opposite, opposite_own, order))
        onward = opposite_own[begin : begin + middle] + opposite[begin : begin + middle]
        back = opposite_own[begin + middle : end] + opposite[begin + middle : end]
        onward, back, order = tie((onward, back, order))
        streams.append((send(onward, up), send(back, down)))
    for turn in range(3):
        for k, (begin, end) in enumerate(SPANS):
            onward, back = streams[k]
            if turn == 0:
                zero = jnp.float32(0)
                onward = lax.pad(onward, zero, ((0, (end - begin) // 2, 0), (0, 0, 0), (0, 0, 0)))
                back = lax.pad(back, zero, (((end - begin) // 2, 0, 0), (0, 0, 0), (0, 0, 0)))
            rest, rest_own, order = tie((rest, rest_own, order))
            at = 2 * turn * UNITS
            onward = rest_own[at + begin : at + end] + rest[at + begin : at + end] + onward
            at += UNITS
            back = rest_own[at + begin : at + end] + rest[at + begin : at + end] + back
            onward, back, order = tie((onward, back, order))
            streams[k] = send(onward, up), send(back, down)

    early = SPANS[0][1] // 2 * (features.shape[0] // RUNS) // size
    lists = block_lists(target_block, source_block, block_count, early)
    partial, kept = early_blocks(lists, near_own, near, streams[0], adjacency, target_blocks)
    partial = late_blocks(partial, lists, near_own, near, streams[1], kept)

    partial = partial.reshape(node_count, 2 * CHIPS, TILE, size)
    parts = combine(lax.all_to_all(partial, "node", 0, 0))
    parts = lax.all_to_all(parts, "feat", 0, 0)
    return second(
        parts, bias_one, self_weight, neigh_weight, bias_two, seed_ids, neighbor_ids
    )


def solution(mesh):
    placed = (
        P("node", "feat"),
        P("node", None, None),
        P("node"),
        P("node"),
        P("node"),
        P("feat", None),
        P(),
        P(),
        P(),
        P(),
        P(("node", "feat")),
        P(("node", "feat"), None),
    )
    return jax.shard_map(
        on_device, mesh=mesh, in_specs=placed, out_specs=P(("node", "feat"), None), check_vma=False
    )
```

```python
import functools

import jax
import jax.numpy as jnp
from jax import lax
from jax.experimental import pallas as pl
from jax.experimental.pallas import tpu as pltpu
from jax.sharding import PartitionSpec as P

T_DEV = 64
CHIPS = 8
TILE = 8
RUNS = 8
SPANS = ((0, 10), (10, 16))
GROUP = 16
NT = (((1,), (1,)), ((), ()))
VMEM = pl.BlockSpec(memory_space=pltpu.VMEM)
SMEM = pl.BlockSpec(memory_space=pltpu.SMEM)

UNITS = 2 * RUNS


def project_kernel(ordered, features, *outs):
    lanes = outs[0].shape[2]
    tile = min(512, lanes)
    for i in range(features.shape[0] // tile):
        rows = features[i * tile : (i + 1) * tile]
        product = lax.dot_general(ordered[...], rows, NT, preferred_element_type=jnp.float32)
        run, at = divmod(i * tile, lanes)
        take = 0
        for out in outs:
            for k in range(out.shape[0] // RUNS):
                unit = k // 2 * UNITS + 2 * run + k % 2
                out[unit, :, at : at + tile] = product[take : take + TILE]
                take += TILE


def project(ordered, features):
    rows, columns = features.shape
    hidden = ordered.shape[0]
    shapes = [
        jax.ShapeDtypeStruct((strips * UNITS, TILE, rows // RUNS), jnp.float32)
        for strips in (1, CHIPS - 1)
    ] * 2
    return pl.pallas_call(
        project_kernel,
        in_specs=[VMEM] * 2,
        out_specs=[VMEM] * 4,
        out_shape=shapes,
        name="project",
        compiler_params=pltpu.CompilerParams(vmem_limit_bytes=8 * 2**20),
        cost_estimate=pl.CostEstimate(
            flops=2 * rows * columns * hidden,
            bytes_accessed=rows * columns * 2 + rows * hidden * 4,
            transcendentals=0,
        ),
    )(ordered, features)


def in_hop_order(layer_one):
    hidden = layer_one.shape[1]
    feat = lax.axis_index("feat")
    row = jnp.arange(hidden, dtype=jnp.int32)
    place = row % (hidden // 2) // (2 * TILE)
    hop = (place + 1) // 2
    hop = CHIPS // 2 + jnp.where(place % 2 == 1, -hop, hop)
    chip = ((feat >> 1) + hop) % CHIPS
    core = ((feat & 1) + (row < hidden // 2)) % 2
    wanted = (chip * 2 + core) * (2 * TILE) + row % (2 * TILE)
    pick = (jnp.arange(hidden, dtype=jnp.int32)[None, :] == wanted[:, None]).astype(jnp.bfloat16)
    return lax.dot_general(pick, layer_one, NT, preferred_element_type=jnp.float32).astype(
        jnp.bfloat16
    )


def lists_kernel(early, count, target, source, out):
    slots = target.shape[1]
    slot = lax.broadcasted_iota(jnp.int32, (1, slots), 1)
    late = (source[...] >= early).astype(jnp.int32)
    key = jnp.where(slot < count[0], late, 2) * slots + slot
    across = jnp.broadcast_to(key, (slots, slots))
    rank = jnp.sum((across.T < across).astype(jnp.float32), axis=0, keepdims=True)
    first = jnp.sum((key < slots).astype(jnp.float32), axis=1, keepdims=True)
    place = 2 * target[...] - target[...] % CHIPS
    row = lax.broadcasted_iota(jnp.int32, (out.shape[0], slots), 0)
    values = jnp.zeros(row.shape, jnp.float32)
    for k, value in enumerate((place, source[...], slot, first, count[0].astype(jnp.float32))):
        if k < 3:
            value = value.astype(jnp.float32)
        values = jnp.where(row == k, value, values)
    at = lax.broadcasted_iota(jnp.int32, (out.shape[1], slots), 0).astype(jnp.float32) == rank
    out[...] = lax.dot_general(
        values.astype(jnp.bfloat16),
        at.astype(jnp.bfloat16),
        NT,
        preferred_element_type=jnp.float32,
    ).astype(jnp.int32)


def block_lists(target_block, source_block, block_count, early):
    slots = target_block.shape[0]
    return pl.pallas_call(
        functools.partial(lists_kernel, early),
        in_specs=[SMEM] + [VMEM] * 2,
        out_specs=VMEM,
        out_shape=jax.ShapeDtypeStruct((TILE, slots + 128), jnp.int32),
        name="block_lists",
        compiler_params=pltpu.CompilerParams(vmem_limit_bytes=4 * 2**20),
    )(block_count, target_block[None, :], source_block[None, :])


def block_products(late, table, own, paired, up, down, adjacency, out, held):
    size = adjacency.shape[1]
    lanes = own.shape[2]
    base = own.shape[0] - UNITS
    begin = SPANS[late][0]
    for b in range(begin // 2 * lanes // size, SPANS[late][1] // 2 * lanes // size):
        run, at = divmod(b * size, lanes)
        at = slice(at, at + size)
        total = jnp.concatenate(
            [
                (own[base + unit, :, at] + paired[base + unit, :, at])
                + (up[unit - begin, :, at] + down[unit - begin, :, at])
                for unit in (2 * run, 2 * run + 1)
            ],
            axis=0,
        )
        upper = total.astype(jnp.bfloat16)
        held[b, : 2 * TILE] = upper
        held[b, 2 * TILE :] = (total - upper.astype(jnp.float32)).astype(jnp.bfloat16)
    start = table[3, 0] if late else 0
    end = table[4 if late else 3, 0]

    def products(first):
        values = []
        for k in range(0, GROUP, 2):
            left = [held[table[1, first + k + j]] for j in range(2)]
            right = [
                adjacency[first - start + k + j if late else table[2, first + k + j]]
                for j in range(2)
            ]
            value = lax.dot_general(
                jnp.concatenate(left, axis=0),
                jnp.concatenate(right, axis=0),
                NT,
                preferred_element_type=jnp.float32,
            )
            rows = 2 * TILE
            values.append(value[:rows, :size] + value[rows : 2 * rows, :size])
            values.append(value[2 * rows : 3 * rows, size:] + value[3 * rows :, size:])
        return values

    def add(first, values):
        for k in range(GROUP):
            place = table[0, first + k]
            value = jnp.where(first + k < end, values[k], 0.0)
            out[place] += value[:TILE]
            out[place + CHIPS] += value[TILE:]

    def whole(i, before):
        after = products(start + i * GROUP)
        add(start + (i - 1) * GROUP, before)
        return after

    groups = (end - start + GROUP - 1) // GROUP
    last = lax.fori_loop(1, groups, whole, products(start))
    add(start + (jnp.maximum(groups, 1) - 1) * GROUP, last)


def early_kernel(table, own, paired, up, down, adjacency, out, kept, held):
    out[...] = jnp.zeros_like(out)
    block_products(0, table, own, paired, up, down, adjacency, out, held)

    def keep(i, carry):
        kept[i - table[3, 0]] = adjacency[table[2, i]]
        return carry

    lax.fori_loop(table[3, 0], table[4, 0], keep, 0)


def late_kernel(before, table, own, paired, up, down, kept, out, held):
    out[...] = before[...]
    block_products(1, table, own, paired, up, down, kept, out, held)


def early_blocks(lists, own, paired, stream, adjacency, target_blocks):
    slots, size, _ = adjacency.shape
    return pl.pallas_call(
        early_kernel,
        in_specs=[SMEM] + [VMEM] * 5,
        out_specs=[VMEM] * 2,
        out_shape=[
            jax.ShapeDtypeStruct((2 * target_blocks, TILE, size), jnp.float32),
            jax.ShapeDtypeStruct((slots + GROUP, size, size), adjacency.dtype),
        ],
        scratch_shapes=[pltpu.VMEM((RUNS * own.shape[2] // size, 4 * TILE, size), jnp.bfloat16)],
        name="early_blocks",
        compiler_params=pltpu.CompilerParams(vmem_limit_bytes=8 * 2**20),
        cost_estimate=pl.CostEstimate(
            flops=4 * slots * size * size * UNITS,
            bytes_accessed=slots * size * size,
            transcendentals=0,
        ),
    )(lists, own, paired, *stream, adjacency)


def late_blocks(before, lists, own, paired, stream, kept):
    slots, size, _ = kept.shape
    return pl.pallas_call(
        late_kernel,
        in_specs=[VMEM, SMEM] + [VMEM] * 5,
        out_specs=VMEM,
        out_shape=jax.ShapeDtypeStruct(before.shape, jnp.float32),
        scratch_shapes=[pltpu.VMEM((RUNS * own.shape[2] // size, 4 * TILE, size), jnp.bfloat16)],
        name="late_blocks",
        compiler_params=pltpu.CompilerParams(vmem_limit_bytes=8 * 2**20),
        cost_estimate=pl.CostEstimate(
            flops=4 * slots * size * size * UNITS,
            bytes_accessed=slots * size * size,
            transcendentals=0,
        ),
    )(before, lists, own, paired, *stream, kept)


def combine_kernel(parts, out):
    size = parts.shape[3]
    low = lax.broadcasted_iota(jnp.int32, (TILE, size), 1) < T_DEV
    for chip in range(CHIPS):
        left, right = parts[0, chip], parts[0, CHIPS + chip]
        for n in range(1, parts.shape[0]):
            left += parts[n, chip]
            right += parts[n, CHIPS + chip]
        out[2 * chip] = jnp.where(low, left, pltpu.roll(right, T_DEV, 1))
        out[2 * chip + 1] = jnp.where(low, pltpu.roll(left, T_DEV, 1), right)


def combine(parts):
    return pl.pallas_call(
        combine_kernel,
        in_specs=[VMEM],
        out_specs=VMEM,
        out_shape=jax.ShapeDtypeStruct(parts.shape[1:], jnp.float32),
        name="combine",
        compiler_params=pltpu.CompilerParams(vmem_limit_bytes=4 * 2**20),
    )(parts)


def second_kernel(parts, bias_one, self_weight, neigh_weight, bias_two, seeds, neighbors, out):
    rows = []
    for k in range(parts.shape[0]):
        rows += [parts[k], pltpu.roll(parts[k], T_DEV, 1)]
    sums = jnp.concatenate(rows, axis=0)
    bias = jnp.broadcast_to(bias_one[...], (sums.shape[1], sums.shape[0])).T
    hidden = jnp.maximum(sums + bias, 0.0).astype(jnp.bfloat16)
    fan, count = neighbors.shape
    positions = lax.broadcasted_iota(jnp.int32, (hidden.shape[1], count), 0)
    pick_self = (positions == seeds[...]).astype(jnp.float32)
    tally = jnp.zeros(positions.shape, jnp.float32)
    for k in range(fan):
        tally += (positions == neighbors[k : k + 1]).astype(jnp.float32)
    picked = lax.dot_general(
        jnp.concatenate([pick_self.T, tally.T / fan], axis=0).astype(jnp.bfloat16),
        hidden,
        NT,
        preferred_element_type=jnp.float32,
    ).astype(jnp.bfloat16)
    out[...] = (
        lax.dot_general(
            picked[:count], self_weight[...], NT, preferred_element_type=jnp.float32
        )
        + lax.dot_general(
            picked[count:], neigh_weight[...], NT, preferred_element_type=jnp.float32
        )
        + bias_two[...]
    )


def second(parts, bias_one, self_weight, neigh_weight, bias_two, seeds, neighbors):
    return pl.pallas_call(
        second_kernel,
        in_specs=[VMEM] * 7,
        out_specs=VMEM,
        out_shape=jax.ShapeDtypeStruct((seeds.shape[0], bias_two.shape[0]), jnp.float32),
        name="second",
        compiler_params=pltpu.CompilerParams(vmem_limit_bytes=8 * 2**20),
    )(
        parts,
        bias_one[None, :],
        self_weight.T,
        neigh_weight.T,
        bias_two[None, :],
        seeds[None, :],
        neighbors.T,
    )


def on_device(
    features,
    adjacency,
    target_block,
    source_block,
    block_count,
    layer_one,
    bias_one,
    self_weight,
    neigh_weight,
    bias_two,
    seed_ids,
    neighbor_ids,
):
    size = adjacency.shape[1]
    node_count = lax.axis_size("node")
    feat_count = lax.axis_size("feat")
    target_blocks = T_DEV * node_count * feat_count // size

    pair = [(i, i ^ 1) for i in range(feat_count)]
    up = [(i, (i + 2) % feat_count) for i in range(feat_count)]
    down = [((i + 2) % feat_count, i) for i in range(feat_count)]

    def send(value, route):
        return lax.ppermute(value, "feat", route)

    tie = lax.optimization_barrier
    opposite, rest, opposite_own, rest_own = project(in_hop_order(layer_one), features)
    opposite, rest = tie((send(opposite, pair), rest))
    rest = send(rest, pair)

    order = block_count
    streams = []
    for begin, end in SPANS:
        middle = (end - begin) // 2
        opposite, opposite_own, order = tie((opposite, opposite_own, order))
        onward = opposite_own[begin : begin + middle] + opposite[begin : begin + middle]
        back = opposite_own[begin + middle : end] + opposite[begin + middle : end]
        onward, back, order = tie((onward, back, order))
        streams.append((send(onward, up), send(back, down)))
    for turn in range(3):
        for k, (begin, end) in enumerate(SPANS):
            onward, back = streams[k]
            if turn == 0:
                zero = jnp.float32(0)
                onward = lax.pad(onward, zero, ((0, (end - begin) // 2, 0), (0, 0, 0), (0, 0, 0)))
                back = lax.pad(back, zero, (((end - begin) // 2, 0, 0), (0, 0, 0), (0, 0, 0)))
            rest, rest_own, order = tie((rest, rest_own, order))
            at = 2 * turn * UNITS
            onward = rest_own[at + begin : at + end] + rest[at + begin : at + end] + onward
            at += UNITS
            back = rest_own[at + begin : at + end] + rest[at + begin : at + end] + back
            onward, back, order = tie((onward, back, order))
            streams[k] = send(onward, up), send(back, down)

    early = SPANS[0][1] // 2 * (features.shape[0] // RUNS) // size
    lists = block_lists(target_block, source_block, block_count, early)
    partial, kept = early_blocks(lists, rest_own, rest, streams[0], adjacency, target_blocks)
    partial = late_blocks(partial, lists, rest_own, rest, streams[1], kept)

    partial = partial.reshape(node_count, 2 * CHIPS, TILE, size)
    parts = combine(lax.all_to_all(partial, "node", 0, 0))
    parts = lax.all_to_all(parts, "feat", 0, 0)
    return second(
        parts, bias_one, self_weight, neigh_weight, bias_two, seed_ids, neighbor_ids
    )


def solution(mesh):
    placed = (
        P("node", "feat"),
        P("node", None, None),
        P("node"),
        P("node"),
        P("node"),
        P("feat", None),
        P(),
        P(),
        P(),
        P(),
        P(("node", "feat")),
        P(("node", "feat"), None),
    )
    return jax.shard_map(
        on_device, mesh=mesh, in_specs=placed, out_specs=P(("node", "feat"), None), check_vma=False
    )
```

```python
import functools

import jax
import jax.numpy as jnp
from jax import lax
from jax.experimental import pallas as pl
from jax.experimental.pallas import tpu as pltpu
from jax.sharding import PartitionSpec as P

T_DEV = 64
CHIPS = 8
TILE = 8
RUNS = 8
SPANS = ((0, 8), (8, 16))
GROUP = 16
NT = (((1,), (1,)), ((), ()))
VMEM = pl.BlockSpec(memory_space=pltpu.VMEM)
SMEM = pl.BlockSpec(memory_space=pltpu.SMEM)

UNITS = 2 * RUNS


def project_kernel(ordered, features, *outs):
    lanes = outs[0].shape[2]
    tile = min(512, lanes)
    for i in range(features.shape[0] // tile):
        rows = features[i * tile : (i + 1) * tile]
        product = lax.dot_general(ordered[...], rows, NT, preferred_element_type=jnp.float32)
        run, at = divmod(i * tile, lanes)
        take = 0
        for out in outs:
            for k in range(out.shape[0] // RUNS):
                unit = k // 2 * UNITS + 2 * run + k % 2
                out[unit, :, at : at + tile] = product[take : take + TILE]
                take += TILE


def project(ordered, features):
    rows, columns = features.shape
    hidden = ordered.shape[0]
    shapes = [
        jax.ShapeDtypeStruct((strips * UNITS, TILE, rows // RUNS), jnp.float32)
        for strips in (1, CHIPS - 1)
    ] * 2
    return pl.pallas_call(
        project_kernel,
        in_specs=[VMEM] * 2,
        out_specs=[VMEM] * 4,
        out_shape=shapes,
        name="project",
        compiler_params=pltpu.CompilerParams(vmem_limit_bytes=8 * 2**20),
        cost_estimate=pl.CostEstimate(
            flops=2 * rows * columns * hidden,
            bytes_accessed=rows * columns * 2 + rows * hidden * 4,
            transcendentals=0,
        ),
    )(ordered, features)


def in_hop_order(layer_one):
    hidden = layer_one.shape[1]
    feat = lax.axis_index("feat")
    row = jnp.arange(hidden, dtype=jnp.int32)
    place = row % (hidden // 2) // (2 * TILE)
    hop = (place + 1) // 2
    hop = CHIPS // 2 + jnp.where(place % 2 == 1, -hop, hop)
    chip = ((feat >> 1) + hop) % CHIPS
    core = ((feat & 1) + (row < hidden // 2)) % 2
    wanted = (chip * 2 + core) * (2 * TILE) + row % (2 * TILE)
    pick = (jnp.arange(hidden, dtype=jnp.int32)[None, :] == wanted[:, None]).astype(jnp.bfloat16)
    return lax.dot_general(pick, layer_one, NT, preferred_element_type=jnp.float32).astype(
        jnp.bfloat16
    )


def lists_kernel(early, count, target, source, out):
    slots = target.shape[1]
    slot = lax.broadcasted_iota(jnp.int32, (1, slots), 1)
    late = (source[...] >= early).astype(jnp.int32)
    key = jnp.where(slot < count[0], late, 2) * slots + slot
    across = jnp.broadcast_to(key, (slots, slots))
    rank = jnp.sum((across.T < across).astype(jnp.float32), axis=0, keepdims=True)
    first = jnp.sum((key < slots).astype(jnp.float32), axis=1, keepdims=True)
    place = 2 * target[...] - target[...] % CHIPS
    row = lax.broadcasted_iota(jnp.int32, (out.shape[0], slots), 0)
    values = jnp.zeros(row.shape, jnp.float32)
    for k, value in enumerate((place, source[...], slot, first, count[0].astype(jnp.float32))):
        if k < 3:
            value = value.astype(jnp.float32)
        values = jnp.where(row == k, value, values)
    at = lax.broadcasted_iota(jnp.int32, (out.shape[1], slots), 0).astype(jnp.float32) == rank
    out[...] = lax.dot_general(
        values.astype(jnp.bfloat16),
        at.astype(jnp.bfloat16),
        NT,
        preferred_element_type=jnp.float32,
    ).astype(jnp.int32)


def block_lists(target_block, source_block, block_count, early):
    slots = target_block.shape[0]
    return pl.pallas_call(
        functools.partial(lists_kernel, early),
        in_specs=[SMEM] + [VMEM] * 2,
        out_specs=VMEM,
        out_shape=jax.ShapeDtypeStruct((TILE, slots + 128), jnp.int32),
        name="block_lists",
        compiler_params=pltpu.CompilerParams(vmem_limit_bytes=4 * 2**20),
    )(block_count, target_block[None, :], source_block[None, :])


def block_products(late, table, own, paired, up, down, adjacency, out, held):
    size = adjacency.shape[1]
    lanes = own.shape[2]
    base = own.shape[0] - UNITS
    begin = SPANS[late][0]
    for b in range(begin // 2 * lanes // size, SPANS[late][1] // 2 * lanes // size):
        run, at = divmod(b * size, lanes)
        at = slice(at, at + size)
        total = jnp.concatenate(
            [
                (own[base + unit, :, at] + paired[base + unit, :, at])
                + (up[unit - begin, :, at] + down[unit - begin, :, at])
                for unit in (2 * run, 2 * run + 1)
            ],
            axis=0,
        )
        upper = total.astype(jnp.bfloat16)
        held[b, : 2 * TILE] = upper
        held[b, 2 * TILE :] = (total - upper.astype(jnp.float32)).astype(jnp.bfloat16)
    start = table[3, 0] if late else 0
    end = table[4 if late else 3, 0]

    def products(first):
        values = []
        for k in range(0, GROUP, 2):
            left = [held[table[1, first + k + j]] for j in range(2)]
            right = [adjacency[table[2, first + k + j]] for j in range(2)]
            value = lax.dot_general(
                jnp.concatenate(left, axis=0),
                jnp.concatenate(right, axis=0),
                NT,
                preferred_element_type=jnp.float32,
            )
            rows = 2 * TILE
            values.append(value[:rows, :size] + value[rows : 2 * rows, :size])
            values.append(value[2 * rows : 3 * rows, size:] + value[3 * rows :, size:])
        return values

    def add(first, values):
        for k in range(GROUP):
            place = table[0, first + k]
            value = jnp.where(first + k < end, values[k], 0.0)
            out[place] += value[:TILE]
            out[place + CHIPS] += value[TILE:]

    def whole(i, before):
        after = products(start + i * GROUP)
        add(start + (i - 1) * GROUP, before)
        return after

    groups = (end - start + GROUP - 1) // GROUP
    last = lax.fori_loop(1, groups, whole, products(start))
    add(start + (jnp.maximum(groups, 1) - 1) * GROUP, last)


def early_kernel(table, own, paired, up, down, adjacency, out, held):
    out[...] = jnp.zeros_like(out)
    block_products(0, table, own, paired, up, down, adjacency, out, held)


def late_kernel(before, table, own, paired, up, down, adjacency, out, held):
    out[...] = before[...]
    block_products(1, table, own, paired, up, down, adjacency, out, held)


def blocks(before, lists, own, paired, stream, adjacency, target_blocks):
    slots, size, _ = adjacency.shape
    late = before is not None
    return pl.pallas_call(
        late_kernel if late else early_kernel,
        in_specs=[VMEM] * late + [SMEM] + [VMEM] * 5,
        out_specs=VMEM,
        out_shape=jax.ShapeDtypeStruct((2 * target_blocks, TILE, size), jnp.float32),
        scratch_shapes=[pltpu.VMEM((RUNS * own.shape[2] // size, 4 * TILE, size), jnp.bfloat16)],
        name="late_blocks" if late else "early_blocks",
        compiler_params=pltpu.CompilerParams(vmem_limit_bytes=8 * 2**20),
        cost_estimate=pl.CostEstimate(
            flops=4 * slots * size * size * UNITS,
            bytes_accessed=slots * size * size,
            transcendentals=0,
        ),
    )(*([before] if late else []), lists, own, paired, *stream, adjacency)


def combine_kernel(parts, out):
    size = parts.shape[3]
    low = lax.broadcasted_iota(jnp.int32, (TILE, size), 1) < T_DEV
    for chip in range(CHIPS):
        left, right = parts[0, chip], parts[0, CHIPS + chip]
        for n in range(1, parts.shape[0]):
            left += parts[n, chip]
            right += parts[n, CHIPS + chip]
        out[2 * chip] = jnp.where(low, left, pltpu.roll(right, T_DEV, 1))
        out[2 * chip + 1] = jnp.where(low, pltpu.roll(left, T_DEV, 1), right)


def combine(parts):
    return pl.pallas_call(
        combine_kernel,
        in_specs=[VMEM],
        out_specs=VMEM,
        out_shape=jax.ShapeDtypeStruct(parts.shape[1:], jnp.float32),
        name="combine",
        compiler_params=pltpu.CompilerParams(vmem_limit_bytes=4 * 2**20),
    )(parts)


def second_kernel(parts, bias_one, self_weight, neigh_weight, bias_two, seeds, neighbors, out):
    rows = []
    for k in range(parts.shape[0]):
        rows += [parts[k], pltpu.roll(parts[k], T_DEV, 1)]
    sums = jnp.concatenate(rows, axis=0)
    bias = jnp.broadcast_to(bias_one[...], (sums.shape[1], sums.shape[0])).T
    hidden = jnp.maximum(sums + bias, 0.0).astype(jnp.bfloat16)
    fan, count = neighbors.shape
    positions = lax.broadcasted_iota(jnp.int32, (hidden.shape[1], count), 0)
    pick_self = (positions == seeds[...]).astype(jnp.float32)
    tally = jnp.zeros(positions.shape, jnp.float32)
    for k in range(fan):
        tally += (positions == neighbors[k : k + 1]).astype(jnp.float32)
    picked = lax.dot_general(
        jnp.concatenate([pick_self.T, tally.T / fan], axis=0).astype(jnp.bfloat16),
        hidden,
        NT,
        preferred_element_type=jnp.float32,
    ).astype(jnp.bfloat16)
    out[...] = (
        lax.dot_general(
            picked[:count], self_weight[...], NT, preferred_element_type=jnp.float32
        )
        + lax.dot_general(
            picked[count:], neigh_weight[...], NT, preferred_element_type=jnp.float32
        )
        + bias_two[...]
    )


def second(parts, bias_one, self_weight, neigh_weight, bias_two, seeds, neighbors):
    return pl.pallas_call(
        second_kernel,
        in_specs=[VMEM] * 7,
        out_specs=VMEM,
        out_shape=jax.ShapeDtypeStruct((seeds.shape[0], bias_two.shape[0]), jnp.float32),
        name="second",
        compiler_params=pltpu.CompilerParams(vmem_limit_bytes=8 * 2**20),
    )(
        parts,
        bias_one[None, :],
        self_weight.T,
        neigh_weight.T,
        bias_two[None, :],
        seeds[None, :],
        neighbors.T,
    )


def on_device(
    features,
    adjacency,
    target_block,
    source_block,
    block_count,
    layer_one,
    bias_one,
    self_weight,
    neigh_weight,
    bias_two,
    seed_ids,
    neighbor_ids,
):
    size = adjacency.shape[1]
    node_count = lax.axis_size("node")
    feat_count = lax.axis_size("feat")
    target_blocks = T_DEV * node_count * feat_count // size

    pair = [(i, i ^ 1) for i in range(feat_count)]
    up = [(i, (i + 2) % feat_count) for i in range(feat_count)]
    down = [((i + 2) % feat_count, i) for i in range(feat_count)]

    def send(value, route):
        return lax.ppermute(value, "feat", route)

    tie = lax.optimization_barrier
    opposite, rest, opposite_own, rest_own = project(in_hop_order(layer_one), features)
    opposite, rest = tie((send(opposite, pair), rest))
    rest = send(rest, pair)

    order = block_count
    streams = []
    for begin, end in SPANS:
        middle = (end - begin) // 2
        opposite, opposite_own, order = tie((opposite, opposite_own, order))
        onward = opposite_own[begin : begin + middle] + opposite[begin : begin + middle]
        back = opposite_own[begin + middle : end] + opposite[begin + middle : end]
        onward, back, order = tie((onward, back, order))
        streams.append((send(onward, up), send(back, down)))
    for turn in range(3):
        for k, (begin, end) in enumerate(SPANS):
            onward, back = streams[k]
            if turn == 0:
                zero = jnp.float32(0)
                onward = lax.pad(onward, zero, ((0, (end - begin) // 2, 0), (0, 0, 0), (0, 0, 0)))
                back = lax.pad(back, zero, (((end - begin) // 2, 0, 0), (0, 0, 0), (0, 0, 0)))
            rest, rest_own, order = tie((rest, rest_own, order))
            at = 2 * turn * UNITS
            onward = rest_own[at + begin : at + end] + rest[at + begin : at + end] + onward
            at += UNITS
            back = rest_own[at + begin : at + end] + rest[at + begin : at + end] + back
            onward, back, order = tie((onward, back, order))
            streams[k] = send(onward, up), send(back, down)

    early = SPANS[0][1] // 2 * (features.shape[0] // RUNS) // size
    lists = block_lists(target_block, source_block, block_count, early)
    partial = None
    for stream in streams:
        partial = blocks(partial, lists, rest_own, rest, stream, adjacency, target_blocks)

    partial = partial.reshape(node_count, 2 * CHIPS, TILE, size)
    parts = combine(lax.all_to_all(partial, "node", 0, 0))
    parts = lax.all_to_all(parts, "feat", 0, 0)
    return second(
        parts, bias_one, self_weight, neigh_weight, bias_two, seed_ids, neighbor_ids
    )


def solution(mesh):
    placed = (
        P("node", "feat"),
        P("node", None, None),
        P("node"),
        P("node"),
        P("node"),
        P("feat", None),
        P(),
        P(),
        P(),
        P(),
        P(("node", "feat")),
        P(("node", "feat"), None),
    )
    return jax.shard_map(
        on_device, mesh=mesh, in_specs=placed, out_specs=P(("node", "feat"), None), check_vma=False
    )
```

```python
import functools

import jax
import jax.numpy as jnp
from jax import lax
from jax.experimental import pallas as pl
from jax.experimental.pallas import tpu as pltpu
from jax.sharding import PartitionSpec as P

T_DEV = 64
CHIPS = 8
TILE = 8
RUNS = 8
GROUP = 16
NT = (((1,), (1,)), ((), ()))
VMEM = pl.BlockSpec(memory_space=pltpu.VMEM)
SMEM = pl.BlockSpec(memory_space=pltpu.SMEM)

UNITS = 2 * RUNS


def project_kernel(ordered, features, *outs):
    lanes = outs[0].shape[2]
    tile = min(512, lanes)
    for i in range(features.shape[0] // tile):
        rows = features[i * tile : (i + 1) * tile]
        product = lax.dot_general(ordered[...], rows, NT, preferred_element_type=jnp.float32)
        run, at = divmod(i * tile, lanes)
        take = 0
        for out in outs:
            for k in range(out.shape[0] // RUNS):
                out[k * RUNS + run, :, at : at + tile] = product[take : take + TILE]
                take += TILE


def project(ordered, features):
    rows, columns = features.shape
    hidden = ordered.shape[0]
    shapes = [
        jax.ShapeDtypeStruct((strips * UNITS, TILE, rows // RUNS), jnp.float32)
        for strips in (1, 2, CHIPS - 3)
    ] * 2
    return pl.pallas_call(
        project_kernel,
        in_specs=[VMEM] * 2,
        out_specs=[VMEM] * 6,
        out_shape=shapes,
        name="project",
        compiler_params=pltpu.CompilerParams(vmem_limit_bytes=8 * 2**20),
        cost_estimate=pl.CostEstimate(
            flops=2 * rows * columns * hidden,
            bytes_accessed=rows * columns * 2 + rows * hidden * 4,
            transcendentals=0,
        ),
    )(ordered, features)


def in_hop_order(layer_one):
    hidden = layer_one.shape[1]
    feat = lax.axis_index("feat")
    row = jnp.arange(hidden, dtype=jnp.int32)
    place = row % (hidden // 2) // (2 * TILE)
    hop = (place + 1) // 2
    hop = CHIPS // 2 + jnp.where(place % 2 == 1, -hop, hop)
    chip = ((feat >> 1) + hop) % CHIPS
    core = ((feat & 1) + (row < hidden // 2)) % 2
    wanted = (chip * 2 + core) * (2 * TILE) + row % (2 * TILE)
    pick = (jnp.arange(hidden, dtype=jnp.int32)[None, :] == wanted[:, None]).astype(jnp.bfloat16)
    return lax.dot_general(pick, layer_one, NT, preferred_element_type=jnp.float32).astype(
        jnp.bfloat16
    )


def blocks_kernel(stream, target, source, count, own, paired, up, down, adjacency, out, held):
    out[...] = jnp.zeros_like(out)
    size = adjacency.shape[1]
    lanes = own.shape[2]
    base = own.shape[0] - UNITS + stream * RUNS
    for b in range(held.shape[0]):
        run, at = divmod(b * size, lanes)
        at = slice(at, at + size)
        total = (own[base + run, :, at] + paired[base + run, :, at]) + (
            up[run, :, at] + down[run, :, at]
        )
        upper = total.astype(jnp.bfloat16).astype(jnp.float32)
        held[b] = jnp.concatenate([upper, total - upper], axis=0).astype(jnp.bfloat16)
    slots = adjacency.shape[0]
    live = count[0]

    def products(first):
        values = []
        for k in range(0, GROUP, 2):
            pair = [jnp.minimum(first + k + j, slots - 1) for j in range(2)]
            value = lax.dot_general(
                jnp.concatenate([held[source[s]] for s in pair], axis=0),
                jnp.concatenate([adjacency[s] for s in pair], axis=0),
                NT,
                preferred_element_type=jnp.float32,
            )
            values.append(value[:TILE, :size] + value[TILE : 2 * TILE, :size])
            values.append(value[2 * TILE : 3 * TILE, size:] + value[3 * TILE :, size:])
        return values

    def add(first, values):
        for k in range(GROUP):
            slot = jnp.minimum(first + k, slots - 1)
            out[target[slot]] += jnp.where(first + k < live, values[k], 0.0)

    def whole(i, before):
        after = products(i * GROUP)
        add((i - 1) * GROUP, before)
        return after

    groups = (live + GROUP - 1) // GROUP
    last = lax.fori_loop(1, groups, whole, products(0))
    add((jnp.maximum(groups, 1) - 1) * GROUP, last)


def blocks(stream, lists, own, paired, sums, adjacency, target_blocks):
    slots, size, _ = adjacency.shape
    return pl.pallas_call(
        functools.partial(blocks_kernel, stream),
        in_specs=[SMEM] * 3 + [VMEM] * 5,
        out_specs=VMEM,
        out_shape=jax.ShapeDtypeStruct((target_blocks, TILE, size), jnp.float32),
        scratch_shapes=[pltpu.VMEM((RUNS * own.shape[2] // size, 2 * TILE, size), jnp.bfloat16)],
        name="first_blocks" if stream == 0 else "second_blocks",
        compiler_params=pltpu.CompilerParams(vmem_limit_bytes=8 * 2**20),
        cost_estimate=pl.CostEstimate(
            flops=4 * slots * size * size * UNITS,
            bytes_accessed=slots * size * size,
            transcendentals=0,
        ),
    )(*lists, own, paired, *sums, adjacency)


def combine_kernel(first, second, out):
    size = first.shape[3]
    low = lax.broadcasted_iota(jnp.int32, (TILE, size), 1) < T_DEV
    for chip in range(CHIPS):
        left, right = first[0, chip], second[0, chip]
        for n in range(1, first.shape[0]):
            left += first[n, chip]
            right += second[n, chip]
        out[2 * chip] = jnp.where(low, left, pltpu.roll(right, T_DEV, 1))
        out[2 * chip + 1] = jnp.where(low, pltpu.roll(left, T_DEV, 1), right)


def combine(first, second):
    return pl.pallas_call(
        combine_kernel,
        in_specs=[VMEM] * 2,
        out_specs=VMEM,
        out_shape=jax.ShapeDtypeStruct((2 * CHIPS, *first.shape[2:]), jnp.float32),
        name="combine",
        compiler_params=pltpu.CompilerParams(vmem_limit_bytes=4 * 2**20),
    )(first, second)


def second_kernel(parts, bias_one, self_weight, neigh_weight, bias_two, seeds, neighbors, out):
    rows = []
    for k in range(parts.shape[0]):
        rows += [parts[k], pltpu.roll(parts[k], T_DEV, 1)]
    sums = jnp.concatenate(rows, axis=0)
    bias = jnp.broadcast_to(bias_one[...], (sums.shape[1], sums.shape[0])).T
    hidden = jnp.maximum(sums + bias, 0.0).astype(jnp.bfloat16)
    fan, count = neighbors.shape
    positions = lax.broadcasted_iota(jnp.int32, (hidden.shape[1], count), 0)
    pick_self = (positions == seeds[...]).astype(jnp.float32)
    tally = jnp.zeros(positions.shape, jnp.float32)
    for k in range(fan):
        tally += (positions == neighbors[k : k + 1]).astype(jnp.float32)
    picked = lax.dot_general(
        jnp.concatenate([pick_self.T, tally.T / fan], axis=0).astype(jnp.bfloat16),
        hidden,
        NT,
        preferred_element_type=jnp.float32,
    ).astype(jnp.bfloat16)
    out[...] = (
        lax.dot_general(
            picked[:count], self_weight[...], NT, preferred_element_type=jnp.float32
        )
        + lax.dot_general(
            picked[count:], neigh_weight[...], NT, preferred_element_type=jnp.float32
        )
        + bias_two[...]
    )


def second(parts, bias_one, self_weight, neigh_weight, bias_two, seeds, neighbors):
    return pl.pallas_call(
        second_kernel,
        in_specs=[VMEM] * 7,
        out_specs=VMEM,
        out_shape=jax.ShapeDtypeStruct((seeds.shape[0], bias_two.shape[0]), jnp.float32),
        name="second",
        compiler_params=pltpu.CompilerParams(vmem_limit_bytes=8 * 2**20),
    )(
        parts,
        bias_one[None, :],
        self_weight.T,
        neigh_weight.T,
        bias_two[None, :],
        seeds[None, :],
        neighbors.T,
    )


def on_device(
    features,
    adjacency,
    target_block,
    source_block,
    block_count,
    layer_one,
    bias_one,
    self_weight,
    neigh_weight,
    bias_two,
    seed_ids,
    neighbor_ids,
):
    size = adjacency.shape[1]
    node_count = lax.axis_size("node")
    feat_count = lax.axis_size("feat")
    target_blocks = T_DEV * node_count * feat_count // size

    pair = [(i, i ^ 1) for i in range(feat_count)]
    up = [(i, (i + 2) % feat_count) for i in range(feat_count)]
    down = [((i + 2) % feat_count, i) for i in range(feat_count)]

    def send(value, route):
        return lax.ppermute(value, "feat", route)

    tie = lax.optimization_barrier
    opposite, three, rest, opposite_own, three_own, rest_own = project(
        in_hop_order(layer_one), features
    )
    opposite, three, rest = tie((send(opposite, pair), three, rest))
    three, rest = send(three, pair), send(rest, pair)

    half = RUNS // 2
    lists = target_block, source_block
    order = block_count
    streams = [None, None]

    def advance(k, turn, order, *parts):
        opposite, opposite_own, three, three_own, rest, rest_own = parts
        if turn == 0:
            opposite, opposite_own, order = tie((opposite, opposite_own, order))
            begin = k * RUNS
            middle = begin + half
            onward = opposite_own[begin:middle] + opposite[begin:middle]
            back = opposite_own[middle : middle + half] + opposite[middle : middle + half]
        else:
            onward, back = streams[k]
            if turn == 1:
                zero = jnp.float32(0)
                onward = lax.pad(onward, zero, ((0, half, 0), (0, 0, 0), (0, 0, 0)))
                back = lax.pad(back, zero, ((half, 0, 0), (0, 0, 0), (0, 0, 0)))
                three, three_own, order = tie((three, three_own, order))
                here, there, at = three_own, three, k * RUNS
            else:
                rest, rest_own, order = tie((rest, rest_own, order))
                here, there, at = rest_own, rest, 2 * (turn - 2) * UNITS + k * RUNS
            onward = here[at : at + RUNS] + there[at : at + RUNS] + onward
            at += UNITS
            back = here[at : at + RUNS] + there[at : at + RUNS] + back
        onward, back, order = tie((onward, back, order))
        streams[k] = send(onward, up), send(back, down)
        return order, opposite, opposite_own, three, three_own, rest, rest_own

    state = order, opposite, opposite_own, three, three_own, rest, rest_own
    for k, turn in ((0, 0), (0, 1), (0, 2), (1, 0), (0, 3), (1, 1)):
        state = advance(k, turn, *state)
    first = blocks(
        0, (*lists, state[0]), rest_own, rest, streams[0], adjacency, target_blocks
    )
    first, order = tie((first, state[0]))
    state = advance(1, 2, order, *state[1:])
    first, order = tie((first, state[0]))
    first = lax.all_to_all(first.reshape(node_count, CHIPS, TILE, size), "node", 0, 0)
    order, *_ = advance(1, 3, order, *state[1:])
    last = blocks(1, (*lists, order), rest_own, rest, streams[1], adjacency, target_blocks)
    last = lax.all_to_all(last.reshape(node_count, CHIPS, TILE, size), "node", 0, 0)

    parts = combine(first, last)
    parts = lax.all_to_all(parts, "feat", 0, 0)
    return second(
        parts, bias_one, self_weight, neigh_weight, bias_two, seed_ids, neighbor_ids
    )


def solution(mesh):
    placed = (
        P("node", "feat"),
        P("node", None, None),
        P("node"),
        P("node"),
        P("node"),
        P("feat", None),
        P(),
        P(),
        P(),
        P(),
        P(("node", "feat")),
        P(("node", "feat"), None),
    )
    return jax.shard_map(
        on_device, mesh=mesh, in_specs=placed, out_specs=P(("node", "feat"), None), check_vma=False
    )
```

```python
import functools

import jax
import jax.numpy as jnp
from jax import lax
from jax.experimental import pallas as pl
from jax.experimental.pallas import tpu as pltpu
from jax.sharding import PartitionSpec as P

T_DEV = 64
CHIPS = 8
TILE = 8
RUNS = 8
SPANS = ((0, 8), (8, 16))
GROUP = 16
NT = (((1,), (1,)), ((), ()))
VMEM = pl.BlockSpec(memory_space=pltpu.VMEM)
SMEM = pl.BlockSpec(memory_space=pltpu.SMEM)

UNITS = 2 * RUNS


def project_kernel(ordered, features, *outs):
    lanes = outs[0].shape[2]
    tile = min(512, lanes)
    for i in range(features.shape[0] // tile):
        rows = features[i * tile : (i + 1) * tile]
        product = lax.dot_general(ordered[...], rows, NT, preferred_element_type=jnp.float32)
        run, at = divmod(i * tile, lanes)
        take = 0
        for out in outs:
            for k in range(out.shape[0] // RUNS):
                if out.shape[0] == UNITS:
                    stream, place = divmod(run, RUNS // 2)
                    unit = place // 2 * RUNS + stream * RUNS // 2 + place % 2 * 2 + k
                else:
                    unit = k // 2 * UNITS + 2 * run + k % 2
                out[unit, :, at : at + tile] = product[take : take + TILE]
                take += TILE


def project(ordered, features):
    rows, columns = features.shape
    hidden = ordered.shape[0]
    shapes = [
        jax.ShapeDtypeStruct((strips * UNITS, TILE, rows // RUNS), jnp.float32)
        for strips in (1, 2, CHIPS - 3)
    ] * 2
    return pl.pallas_call(
        project_kernel,
        in_specs=[VMEM] * 2,
        out_specs=[VMEM] * 6,
        out_shape=shapes,
        name="project",
        compiler_params=pltpu.CompilerParams(vmem_limit_bytes=8 * 2**20),
        cost_estimate=pl.CostEstimate(
            flops=2 * rows * columns * hidden,
            bytes_accessed=rows * columns * 2 + rows * hidden * 4,
            transcendentals=0,
        ),
    )(ordered, features)


def in_hop_order(layer_one):
    hidden = layer_one.shape[1]
    feat = lax.axis_index("feat")
    row = jnp.arange(hidden, dtype=jnp.int32)
    place = row % (hidden // 2) // (2 * TILE)
    hop = (place + 1) // 2
    hop = CHIPS // 2 + jnp.where(place % 2 == 1, -hop, hop)
    chip = ((feat >> 1) + hop) % CHIPS
    core = ((feat & 1) + (row < hidden // 2)) % 2
    wanted = (chip * 2 + core) * (2 * TILE) + row % (2 * TILE)
    pick = (jnp.arange(hidden, dtype=jnp.int32)[None, :] == wanted[:, None]).astype(jnp.bfloat16)
    return lax.dot_general(pick, layer_one, NT, preferred_element_type=jnp.float32).astype(
        jnp.bfloat16
    )


def lists_kernel(early, count, target, source, out):
    slots = target.shape[1]
    slot = lax.broadcasted_iota(jnp.int32, (1, slots), 1)
    late = (source[...] >= early).astype(jnp.int32)
    key = jnp.where(slot < count[0], late, 2) * slots + slot
    across = jnp.broadcast_to(key, (slots, slots))
    rank = jnp.sum((across.T < across).astype(jnp.float32), axis=0, keepdims=True)
    first = jnp.sum((key < slots).astype(jnp.float32), axis=1, keepdims=True)
    place = 2 * target[...] - target[...] % CHIPS
    row = lax.broadcasted_iota(jnp.int32, (out.shape[0], slots), 0)
    values = jnp.zeros(row.shape, jnp.float32)
    for k, value in enumerate((place, source[...], slot, first, count[0].astype(jnp.float32))):
        if k < 3:
            value = value.astype(jnp.float32)
        values = jnp.where(row == k, value, values)
    at = lax.broadcasted_iota(jnp.int32, (out.shape[1], slots), 0).astype(jnp.float32) == rank
    out[...] = lax.dot_general(
        values.astype(jnp.bfloat16),
        at.astype(jnp.bfloat16),
        NT,
        preferred_element_type=jnp.float32,
    ).astype(jnp.int32)


def block_lists(target_block, source_block, block_count, early):
    slots = target_block.shape[0]
    return pl.pallas_call(
        functools.partial(lists_kernel, early),
        in_specs=[SMEM] + [VMEM] * 2,
        out_specs=VMEM,
        out_shape=jax.ShapeDtypeStruct((TILE, slots + 128), jnp.int32),
        name="block_lists",
        compiler_params=pltpu.CompilerParams(vmem_limit_bytes=4 * 2**20),
    )(block_count, target_block[None, :], source_block[None, :])


def block_products(late, table, own, paired, up, down, adjacency, out, held):
    size = adjacency.shape[1]
    lanes = own.shape[2]
    base = own.shape[0] - UNITS
    begin = SPANS[late][0]
    for b in range(begin // 2 * lanes // size, SPANS[late][1] // 2 * lanes // size):
        run, at = divmod(b * size, lanes)
        at = slice(at, at + size)
        total = jnp.concatenate(
            [
                (own[base + unit, :, at] + paired[base + unit, :, at])
                + (up[unit - begin, :, at] + down[unit - begin, :, at])
                for unit in (2 * run, 2 * run + 1)
            ],
            axis=0,
        )
        upper = total.astype(jnp.bfloat16)
        held[b, : 2 * TILE] = upper
        held[b, 2 * TILE :] = (total - upper.astype(jnp.float32)).astype(jnp.bfloat16)
    start = table[3, 0] if late else 0
    end = table[4 if late else 3, 0]

    def products(first):
        values = []
        for k in range(0, GROUP, 2):
            left = [held[table[1, first + k + j]] for j in range(2)]
            right = [adjacency[table[2, first + k + j]] for j in range(2)]
            value = lax.dot_general(
                jnp.concatenate(left, axis=0),
                jnp.concatenate(right, axis=0),
                NT,
                preferred_element_type=jnp.float32,
            )
            rows = 2 * TILE
            values.append(value[:rows, :size] + value[rows : 2 * rows, :size])
            values.append(value[2 * rows : 3 * rows, size:] + value[3 * rows :, size:])
        return values

    def add(first, values):
        for k in range(GROUP):
            place = table[0, first + k]
            value = jnp.where(first + k < end, values[k], 0.0)
            out[place] += value[:TILE]
            out[place + CHIPS] += value[TILE:]

    def whole(i, before):
        after = products(start + i * GROUP)
        add(start + (i - 1) * GROUP, before)
        return after

    groups = (end - start + GROUP - 1) // GROUP
    last = lax.fori_loop(1, groups, whole, products(start))
    add(start + (jnp.maximum(groups, 1) - 1) * GROUP, last)


def early_kernel(table, own, paired, up, down, adjacency, out, held):
    out[...] = jnp.zeros_like(out)
    block_products(0, table, own, paired, up, down, adjacency, out, held)


def late_kernel(before, table, own, paired, up, down, adjacency, out, held):
    out[...] = before[...]
    block_products(1, table, own, paired, up, down, adjacency, out, held)


def blocks(before, lists, own, paired, stream, adjacency, target_blocks):
    slots, size, _ = adjacency.shape
    late = before is not None
    return pl.pallas_call(
        late_kernel if late else early_kernel,
        in_specs=[VMEM] * late + [SMEM] + [VMEM] * 5,
        out_specs=VMEM,
        out_shape=jax.ShapeDtypeStruct((2 * target_blocks, TILE, size), jnp.float32),
        scratch_shapes=[pltpu.VMEM((RUNS * own.shape[2] // size, 4 * TILE, size), jnp.bfloat16)],
        name="late_blocks" if late else "early_blocks",
        compiler_params=pltpu.CompilerParams(vmem_limit_bytes=8 * 2**20),
        cost_estimate=pl.CostEstimate(
            flops=4 * slots * size * size * UNITS,
            bytes_accessed=slots * size * size,
            transcendentals=0,
        ),
    )(*([before] if late else []), lists, own, paired, *stream, adjacency)


def combine_kernel(parts, out):
    size = parts.shape[3]
    low = lax.broadcasted_iota(jnp.int32, (TILE, size), 1) < T_DEV
    for chip in range(CHIPS):
        left, right = parts[0, chip], parts[0, CHIPS + chip]
        for n in range(1, parts.shape[0]):
            left += parts[n, chip]
            right += parts[n, CHIPS + chip]
        out[2 * chip] = jnp.where(low, left, pltpu.roll(right, T_DEV, 1))
        out[2 * chip + 1] = jnp.where(low, pltpu.roll(left, T_DEV, 1), right)


def combine(parts):
    return pl.pallas_call(
        combine_kernel,
        in_specs=[VMEM],
        out_specs=VMEM,
        out_shape=jax.ShapeDtypeStruct(parts.shape[1:], jnp.float32),
        name="combine",
        compiler_params=pltpu.CompilerParams(vmem_limit_bytes=4 * 2**20),
    )(parts)


def second_kernel(parts, bias_one, self_weight, neigh_weight, bias_two, seeds, neighbors, out):
    rows = []
    for k in range(parts.shape[0]):
        rows += [parts[k], pltpu.roll(parts[k], T_DEV, 1)]
    sums = jnp.concatenate(rows, axis=0)
    bias = jnp.broadcast_to(bias_one[...], (sums.shape[1], sums.shape[0])).T
    hidden = jnp.maximum(sums + bias, 0.0).astype(jnp.bfloat16)
    fan, count = neighbors.shape
    positions = lax.broadcasted_iota(jnp.int32, (hidden.shape[1], count), 0)
    pick_self = (positions == seeds[...]).astype(jnp.float32)
    tally = jnp.zeros(positions.shape, jnp.float32)
    for k in range(fan):
        tally += (positions == neighbors[k : k + 1]).astype(jnp.float32)
    picked = lax.dot_general(
        jnp.concatenate([pick_self.T, tally.T / fan], axis=0).astype(jnp.bfloat16),
        hidden,
        NT,
        preferred_element_type=jnp.float32,
    ).astype(jnp.bfloat16)
    out[...] = (
        lax.dot_general(
            picked[:count], self_weight[...], NT, preferred_element_type=jnp.float32
        )
        + lax.dot_general(
            picked[count:], neigh_weight[...], NT, preferred_element_type=jnp.float32
        )
        + bias_two[...]
    )


def second(parts, bias_one, self_weight, neigh_weight, bias_two, seeds, neighbors):
    return pl.pallas_call(
        second_kernel,
        in_specs=[VMEM] * 7,
        out_specs=VMEM,
        out_shape=jax.ShapeDtypeStruct((seeds.shape[0], bias_two.shape[0]), jnp.float32),
        name="second",
        compiler_params=pltpu.CompilerParams(vmem_limit_bytes=8 * 2**20),
    )(
        parts,
        bias_one[None, :],
        self_weight.T,
        neigh_weight.T,
        bias_two[None, :],
        seeds[None, :],
        neighbors.T,
    )


def on_device(
    features,
    adjacency,
    target_block,
    source_block,
    block_count,
    layer_one,
    bias_one,
    self_weight,
    neigh_weight,
    bias_two,
    seed_ids,
    neighbor_ids,
):
    size = adjacency.shape[1]
    node_count = lax.axis_size("node")
    feat_count = lax.axis_size("feat")
    target_blocks = T_DEV * node_count * feat_count // size

    pair = [(i, i ^ 1) for i in range(feat_count)]
    up = [(i, (i + 2) % feat_count) for i in range(feat_count)]
    down = [((i + 2) % feat_count, i) for i in range(feat_count)]

    def send(value, route):
        return lax.ppermute(value, "feat", route)

    tie = lax.optimization_barrier
    opposite, three, rest, opposite_own, three_own, rest_own = project(
        in_hop_order(layer_one), features
    )
    opposite, three = tie((send(opposite, pair), three))
    three = send(three, pair)

    half = RUNS // 2
    onward = send(opposite_own[:RUNS] + opposite[:RUNS], up)
    back = send(opposite_own[RUNS:] + opposite[RUNS:], down)
    onward, back, three, rest = tie((onward, back, three, rest))
    rest = send(rest, pair)
    streams = [(onward[:half], back[:half]), (onward[half:], back[half:])]
    order = block_count
    for turn in range(3):
        for k, (begin, end) in enumerate(SPANS):
            onward, back = streams[k]
            if turn == 0:
                zero = jnp.float32(0)
                onward = lax.pad(onward, zero, ((0, half, 0), (0, 0, 0), (0, 0, 0)))
                back = lax.pad(back, zero, ((half, 0, 0), (0, 0, 0), (0, 0, 0)))
                three, three_own, order = tie((three, three_own, order))
                here, there, at = three_own, three, 0
            else:
                rest, rest_own, order = tie((rest, rest_own, order))
                here, there, at = rest_own, rest, 2 * (turn - 1) * UNITS
            onward = here[at + begin : at + end] + there[at + begin : at + end] + onward
            at += UNITS
            back = here[at + begin : at + end] + there[at + begin : at + end] + back
            onward, back, order = tie((onward, back, order))
            streams[k] = send(onward, up), send(back, down)

    early = SPANS[0][1] // 2 * (features.shape[0] // RUNS) // size
    lists = block_lists(target_block, source_block, order, early)
    partial = None
    for stream in streams:
        partial = blocks(partial, lists, rest_own, rest, stream, adjacency, target_blocks)

    partial = partial.reshape(node_count, 2 * CHIPS, TILE, size)
    parts = combine(lax.all_to_all(partial, "node", 0, 0))
    parts = lax.all_to_all(parts, "feat", 0, 0)
    return second(
        parts, bias_one, self_weight, neigh_weight, bias_two, seed_ids, neighbor_ids
    )


def solution(mesh):
    placed = (
        P("node", "feat"),
        P("node", None, None),
        P("node"),
        P("node"),
        P("node"),
        P("feat", None),
        P(),
        P(),
        P(),
        P(),
        P(("node", "feat")),
        P(("node", "feat"), None),
    )
    return jax.shard_map(
        on_device, mesh=mesh, in_specs=placed, out_specs=P(("node", "feat"), None), check_vma=False
    )
```

```python
import functools

import jax
import jax.numpy as jnp
from jax import lax
from jax.experimental import pallas as pl
from jax.experimental.pallas import tpu as pltpu
from jax.sharding import PartitionSpec as P

T_DEV = 64
CHIPS = 8
TILE = 8
RUNS = 8
SPANS = ((0, 10), (10, 16))
GROUP = 16
NT = (((1,), (1,)), ((), ()))
VMEM = pl.BlockSpec(memory_space=pltpu.VMEM)
SMEM = pl.BlockSpec(memory_space=pltpu.SMEM)

UNITS = 2 * RUNS


def project_kernel(ordered, features, *outs):
    lanes = outs[0].shape[2]
    tile = min(512, lanes)
    for i in range(features.shape[0] // tile):
        rows = features[i * tile : (i + 1) * tile]
        product = lax.dot_general(ordered[...], rows, NT, preferred_element_type=jnp.float32)
        run, at = divmod(i * tile, lanes)
        take = 0
        for out in outs:
            for k in range(out.shape[0] // RUNS):
                unit = k // 2 * UNITS + 2 * run + k % 2
                out[unit, :, at : at + tile] = product[take : take + TILE]
                take += TILE


def project(ordered, features):
    rows, columns = features.shape
    hidden = ordered.shape[0]
    shapes = [
        jax.ShapeDtypeStruct((strips * UNITS, TILE, rows // RUNS), jnp.float32)
        for strips in (1, CHIPS - 1)
    ] * 2
    return pl.pallas_call(
        project_kernel,
        in_specs=[VMEM] * 2,
        out_specs=[VMEM] * 4,
        out_shape=shapes,
        name="project",
        compiler_params=pltpu.CompilerParams(vmem_limit_bytes=8 * 2**20),
        cost_estimate=pl.CostEstimate(
            flops=2 * rows * columns * hidden,
            bytes_accessed=rows * columns * 2 + rows * hidden * 4,
            transcendentals=0,
        ),
    )(ordered, features)


def in_hop_order(layer_one):
    hidden = layer_one.shape[1]
    feat = lax.axis_index("feat")
    row = jnp.arange(hidden, dtype=jnp.int32)
    place = row % (hidden // 2) // (2 * TILE)
    hop = (place + 1) // 2
    hop = CHIPS // 2 + jnp.where(place % 2 == 1, -hop, hop)
    chip = ((feat >> 1) + hop) % CHIPS
    core = ((feat & 1) + (row < hidden // 2)) % 2
    wanted = (chip * 2 + core) * (2 * TILE) + row % (2 * TILE)
    pick = (jnp.arange(hidden, dtype=jnp.int32)[None, :] == wanted[:, None]).astype(jnp.bfloat16)
    return lax.dot_general(pick, layer_one, NT, preferred_element_type=jnp.float32).astype(
        jnp.bfloat16
    )


def lists_kernel(early, count, target, source, out):
    slots = target.shape[1]
    slot = lax.broadcasted_iota(jnp.int32, (1, slots), 1)
    late = (source[...] >= early).astype(jnp.int32)
    key = jnp.where(slot < count[0], late, 2) * slots + slot
    across = jnp.broadcast_to(key, (slots, slots))
    rank = jnp.sum((across.T < across).astype(jnp.float32), axis=0, keepdims=True)
    first = jnp.sum((key < slots).astype(jnp.float32), axis=1, keepdims=True)
    place = 2 * target[...] - target[...] % CHIPS
    row = lax.broadcasted_iota(jnp.int32, (out.shape[0], slots), 0)
    values = jnp.zeros(row.shape, jnp.float32)
    for k, value in enumerate((place, source[...], slot, first, count[0].astype(jnp.float32))):
        if k < 3:
            value = value.astype(jnp.float32)
        values = jnp.where(row == k, value, values)
    at = lax.broadcasted_iota(jnp.int32, (out.shape[1], slots), 0).astype(jnp.float32) == rank
    out[...] = lax.dot_general(
        values.astype(jnp.bfloat16),
        at.astype(jnp.bfloat16),
        NT,
        preferred_element_type=jnp.float32,
    ).astype(jnp.int32)


def block_lists(target_block, source_block, block_count, early):
    slots = target_block.shape[0]
    return pl.pallas_call(
        functools.partial(lists_kernel, early),
        in_specs=[SMEM] + [VMEM] * 2,
        out_specs=VMEM,
        out_shape=jax.ShapeDtypeStruct((TILE, slots + 128), jnp.int32),
        name="block_lists",
        compiler_params=pltpu.CompilerParams(vmem_limit_bytes=4 * 2**20),
    )(block_count, target_block[None, :], source_block[None, :])


def block_products(late, table, own, paired, up, down, adjacency, out, held):
    size = adjacency.shape[1]
    lanes = own.shape[2]
    base = own.shape[0] - UNITS
    begin = SPANS[late][0]
    for b in range(begin // 2 * lanes // size, SPANS[late][1] // 2 * lanes // size):
        run, at = divmod(b * size, lanes)
        at = slice(at, at + size)
        total = jnp.concatenate(
            [
                (own[base + unit, :, at] + paired[base + unit, :, at])
                + (up[unit - begin, :, at] + down[unit - begin, :, at])
                for unit in (2 * run, 2 * run + 1)
            ],
            axis=0,
        )
        upper = total.astype(jnp.bfloat16)
        held[b, : 2 * TILE] = upper
        held[b, 2 * TILE :] = (total - upper.astype(jnp.float32)).astype(jnp.bfloat16)
    start = table[3, 0] if late else 0
    end = table[4 if late else 3, 0]

    def products(first):
        values = []
        for k in range(0, GROUP, 2):
            left = [held[table[1, first + k + j]] for j in range(2)]
            right = [adjacency[table[2, first + k + j]] for j in range(2)]
            value = lax.dot_general(
                jnp.concatenate(left, axis=0),
                jnp.concatenate(right, axis=0),
                NT,
                preferred_element_type=jnp.float32,
            )
            rows = 2 * TILE
            values.append(value[:rows, :size] + value[rows : 2 * rows, :size])
            values.append(value[2 * rows : 3 * rows, size:] + value[3 * rows :, size:])
        return values

    def add(first, values):
        for k in range(GROUP):
            place = table[0, first + k]
            value = jnp.where(first + k < end, values[k], 0.0)
            out[place] += value[:TILE]
            out[place + CHIPS] += value[TILE:]

    def whole(i, before):
        after = products(start + i * GROUP)
        add(start + (i - 1) * GROUP, before)
        return after

    groups = (end - start + GROUP - 1) // GROUP
    last = lax.fori_loop(1, groups, whole, products(start))
    add(start + (jnp.maximum(groups, 1) - 1) * GROUP, last)


def early_kernel(table, own, paired, up, down, adjacency, out, held):
    out[...] = jnp.zeros_like(out)
    block_products(0, table, own, paired, up, down, adjacency, out, held)


def late_kernel(before, table, own, paired, up, down, adjacency, out, held):
    out[...] = before[...]
    block_products(1, table, own, paired, up, down, adjacency, out, held)


def blocks(before, lists, own, paired, stream, adjacency, target_blocks):
    slots, size, _ = adjacency.shape
    late = before is not None
    return pl.pallas_call(
        late_kernel if late else early_kernel,
        in_specs=[VMEM] * late + [SMEM] + [VMEM] * 5,
        out_specs=VMEM,
        out_shape=jax.ShapeDtypeStruct((2 * target_blocks, TILE, size), jnp.float32),
        scratch_shapes=[pltpu.VMEM((RUNS * own.shape[2] // size, 4 * TILE, size), jnp.bfloat16)],
        name="late_blocks" if late else "early_blocks",
        compiler_params=pltpu.CompilerParams(vmem_limit_bytes=8 * 2**20),
        cost_estimate=pl.CostEstimate(
            flops=4 * slots * size * size * UNITS,
            bytes_accessed=slots * size * size,
            transcendentals=0,
        ),
    )(*([before] if late else []), lists, own, paired, *stream, adjacency)


def combine_kernel(parts, out):
    size = parts.shape[3]
    low = lax.broadcasted_iota(jnp.int32, (TILE, size), 1) < T_DEV
    for chip in range(CHIPS):
        left, right = parts[0, chip], parts[0, CHIPS + chip]
        for n in range(1, parts.shape[0]):
            left += parts[n, chip]
            right += parts[n, CHIPS + chip]
        out[2 * chip] = jnp.where(low, left, pltpu.roll(right, T_DEV, 1))
        out[2 * chip + 1] = jnp.where(low, pltpu.roll(left, T_DEV, 1), right)


def combine(parts):
    return pl.pallas_call(
        combine_kernel,
        in_specs=[VMEM],
        out_specs=VMEM,
        out_shape=jax.ShapeDtypeStruct(parts.shape[1:], jnp.float32),
        name="combine",
        compiler_params=pltpu.CompilerParams(vmem_limit_bytes=4 * 2**20),
    )(parts)


def second_kernel(parts, bias_one, self_weight, neigh_weight, bias_two, seeds, neighbors, out):
    rows = []
    for k in range(parts.shape[0]):
        rows += [parts[k], pltpu.roll(parts[k], T_DEV, 1)]
    sums = jnp.concatenate(rows, axis=0)
    bias = jnp.broadcast_to(bias_one[...], (sums.shape[1], sums.shape[0])).T
    hidden = jnp.maximum(sums + bias, 0.0).astype(jnp.bfloat16)
    fan, count = neighbors.shape
    positions = lax.broadcasted_iota(jnp.int32, (hidden.shape[1], count), 0)
    pick_self = (positions == seeds[...]).astype(jnp.float32)
    tally = jnp.zeros(positions.shape, jnp.float32)
    for k in range(fan):
        tally += (positions == neighbors[k : k + 1]).astype(jnp.float32)
    picked = lax.dot_general(
        jnp.concatenate([pick_self.T, tally.T / fan], axis=0).astype(jnp.bfloat16),
        hidden,
        NT,
        preferred_element_type=jnp.float32,
    ).astype(jnp.bfloat16)
    out[...] = (
        lax.dot_general(
            picked[:count], self_weight[...], NT, preferred_element_type=jnp.float32
        )
        + lax.dot_general(
            picked[count:], neigh_weight[...], NT, preferred_element_type=jnp.float32
        )
        + bias_two[...]
    )


def second(parts, bias_one, self_weight, neigh_weight, bias_two, seeds, neighbors):
    return pl.pallas_call(
        second_kernel,
        in_specs=[VMEM] * 7,
        out_specs=VMEM,
        out_shape=jax.ShapeDtypeStruct((seeds.shape[0], bias_two.shape[0]), jnp.float32),
        name="second",
        compiler_params=pltpu.CompilerParams(vmem_limit_bytes=8 * 2**20),
    )(
        parts,
        bias_one[None, :],
        self_weight.T,
        neigh_weight.T,
        bias_two[None, :],
        seeds[None, :],
        neighbors.T,
    )


def on_device(
    features,
    adjacency,
    target_block,
    source_block,
    block_count,
    layer_one,
    bias_one,
    self_weight,
    neigh_weight,
    bias_two,
    seed_ids,
    neighbor_ids,
):
    size = adjacency.shape[1]
    node_count = lax.axis_size("node")
    feat_count = lax.axis_size("feat")
    target_blocks = T_DEV * node_count * feat_count // size

    pair = [(i, i ^ 1) for i in range(feat_count)]
    up = [(i, (i + 2) % feat_count) for i in range(feat_count)]
    down = [((i + 2) % feat_count, i) for i in range(feat_count)]

    def send(value, route):
        return lax.ppermute(value, "feat", route)

    tie = lax.optimization_barrier
    opposite, rest, opposite_own, rest_own = project(in_hop_order(layer_one), features)
    opposite, rest = tie((send(opposite, pair), rest))
    rest = send(rest, pair)

    order = block_count
    streams = []
    for begin, end in SPANS:
        middle = (end - begin) // 2
        opposite, opposite_own, order = tie((opposite, opposite_own, order))
        onward = opposite_own[begin : begin + middle] + opposite[begin : begin + middle]
        back = opposite_own[begin + middle : end] + opposite[begin + middle : end]
        onward, back, order = tie((onward, back, order))
        streams.append((send(onward, up), send(back, down)))
    for turn in range(3):
        for k, (begin, end) in enumerate(SPANS):
            onward, back = streams[k]
            if turn == 0:
                zero = jnp.float32(0)
                onward = lax.pad(onward, zero, ((0, (end - begin) // 2, 0), (0, 0, 0), (0, 0, 0)))
                back = lax.pad(back, zero, (((end - begin) // 2, 0, 0), (0, 0, 0), (0, 0, 0)))
            rest, rest_own, order = tie((rest, rest_own, order))
            at = 2 * turn * UNITS
            onward = rest_own[at + begin : at + end] + rest[at + begin : at + end] + onward
            at += UNITS
            back = rest_own[at + begin : at + end] + rest[at + begin : at + end] + back
            onward, back, order = tie((onward, back, order))
            streams[k] = send(onward, up), send(back, down)

    early = SPANS[0][1] // 2 * (features.shape[0] // RUNS) // size
    lists = block_lists(target_block, source_block, block_count, early)
    partial = None
    for stream in streams:
        partial = blocks(partial, lists, rest_own, rest, stream, adjacency, target_blocks)

    partial = partial.reshape(node_count, 2 * CHIPS, TILE, size)
    parts = combine(lax.all_to_all(partial, "node", 0, 0))
    parts = lax.all_to_all(parts, "feat", 0, 0)
    return second(
        parts, bias_one, self_weight, neigh_weight, bias_two, seed_ids, neighbor_ids
    )


def solution(mesh):
    placed = (
        P("node", "feat"),
        P("node", None, None),
        P("node"),
        P("node"),
        P("node"),
        P("feat", None),
        P(),
        P(),
        P(),
        P(),
        P(("node", "feat")),
        P(("node", "feat"), None),
    )
    return jax.shard_map(
        on_device, mesh=mesh, in_specs=placed, out_specs=P(("node", "feat"), None), check_vma=False
    )
```

```python
import functools

import jax
import jax.numpy as jnp
from jax import lax
from jax.experimental import pallas as pl
from jax.experimental.pallas import tpu as pltpu
from jax.sharding import PartitionSpec as P

T_DEV = 64
CHIPS = 8
TILE = 8
RUNS = 8
SPANS = ((0, 10), (10, 16))
GROUP = 16
NT = (((1,), (1,)), ((), ()))
VMEM = pl.BlockSpec(memory_space=pltpu.VMEM)
SMEM = pl.BlockSpec(memory_space=pltpu.SMEM)

UNITS = 2 * RUNS


def project_kernel(first, ordered, features, *outs):
    hidden = ordered.shape[0]
    lanes = outs[0].shape[2]
    tile = min(512, lanes)
    width = 2 * TILE
    strips = 1 if first else CHIPS - 1
    rows = [
        ordered[half + (0 if first else width) : half + (width if first else hidden // 2)]
        for half in (0, hidden // 2)
    ]
    rows = jnp.concatenate(rows, axis=0)
    for i in range(features.shape[0] // tile):
        product = lax.dot_general(
            rows, features[i * tile : (i + 1) * tile], NT, preferred_element_type=jnp.float32
        )
        run, at = divmod(i * tile, lanes)
        at = slice(at, at + tile)
        take = 0
        for core in range(2):
            for strip in range(strips):
                for k in range(2):
                    unit = 2 * run + k
                    if first:
                        stream = int(unit >= SPANS[1][0])
                        out, unit = outs[2 * core + stream], unit - SPANS[stream][0]
                    else:
                        out, unit = outs[core], strip * UNITS + unit
                    out[unit, :, at] = product[take : take + TILE]
                    take += TILE


def project(first, ordered, features):
    rows, columns = features.shape
    hidden = ordered.shape[0]
    units = [end - begin for begin, end in SPANS] if first else [(CHIPS - 1) * UNITS]
    shapes = [
        jax.ShapeDtypeStruct((count, TILE, rows // RUNS), jnp.float32) for count in units
    ] * 2
    return pl.pallas_call(
        functools.partial(project_kernel, first),
        in_specs=[VMEM] * 2,
        out_specs=[VMEM] * len(shapes),
        out_shape=shapes,
        name="project_first" if first else "project_rest",
        compiler_params=pltpu.CompilerParams(vmem_limit_bytes=8 * 2**20),
        cost_estimate=pl.CostEstimate(
            flops=2 * rows * columns * hidden,
            bytes_accessed=rows * columns * 2,
            transcendentals=0,
        ),
    )(ordered, features)


def in_hop_order(layer_one):
    hidden = layer_one.shape[1]
    feat = lax.axis_index("feat")
    row = jnp.arange(hidden, dtype=jnp.int32)
    place = row % (hidden // 2) // (2 * TILE)
    hop = (place + 1) // 2
    hop = CHIPS // 2 + jnp.where(place % 2 == 1, -hop, hop)
    chip = ((feat >> 1) + hop) % CHIPS
    core = ((feat & 1) + (row < hidden // 2)) % 2
    wanted = (chip * 2 + core) * (2 * TILE) + row % (2 * TILE)
    pick = (jnp.arange(hidden, dtype=jnp.int32)[None, :] == wanted[:, None]).astype(jnp.bfloat16)
    return lax.dot_general(pick, layer_one, NT, preferred_element_type=jnp.float32).astype(
        jnp.bfloat16
    )


def lists_kernel(early, count, target, source, out):
    slots = target.shape[1]
    slot = lax.broadcasted_iota(jnp.int32, (1, slots), 1)
    late = (source[...] >= early).astype(jnp.int32)
    key = jnp.where(slot < count[0], late, 2) * slots + slot
    across = jnp.broadcast_to(key, (slots, slots))
    rank = jnp.sum((across.T < across).astype(jnp.float32), axis=0, keepdims=True)
    first = jnp.sum((key < slots).astype(jnp.float32), axis=1, keepdims=True)
    place = 2 * target[...] - target[...] % CHIPS
    row = lax.broadcasted_iota(jnp.int32, (out.shape[0], slots), 0)
    values = jnp.zeros(row.shape, jnp.float32)
    for k, value in enumerate((place, source[...], slot, first, count[0].astype(jnp.float32))):
        if k < 3:
            value = value.astype(jnp.float32)
        values = jnp.where(row == k, value, values)
    at = lax.broadcasted_iota(jnp.int32, (out.shape[1], slots), 0).astype(jnp.float32) == rank
    out[...] = lax.dot_general(
        values.astype(jnp.bfloat16),
        at.astype(jnp.bfloat16),
        NT,
        preferred_element_type=jnp.float32,
    ).astype(jnp.int32)


def block_lists(target_block, source_block, block_count, early):
    slots = target_block.shape[0]
    return pl.pallas_call(
        functools.partial(lists_kernel, early),
        in_specs=[SMEM] + [VMEM] * 2,
        out_specs=VMEM,
        out_shape=jax.ShapeDtypeStruct((TILE, slots + 128), jnp.int32),
        name="block_lists",
        compiler_params=pltpu.CompilerParams(vmem_limit_bytes=4 * 2**20),
    )(block_count, target_block[None, :], source_block[None, :])


def block_products(late, table, own, paired, up, down, adjacency, out, held):
    size = adjacency.shape[1]
    lanes = own.shape[2]
    base = own.shape[0] - UNITS
    begin = SPANS[late][0]
    for b in range(begin // 2 * lanes // size, SPANS[late][1] // 2 * lanes // size):
        run, at = divmod(b * size, lanes)
        at = slice(at, at + size)
        total = jnp.concatenate(
            [
                (own[base + unit, :, at] + paired[base + unit, :, at])
                + (up[unit - begin, :, at] + down[unit - begin, :, at])
                for unit in (2 * run, 2 * run + 1)
            ],
            axis=0,
        )
        upper = total.astype(jnp.bfloat16)
        held[b, : 2 * TILE] = upper
        held[b, 2 * TILE :] = (total - upper.astype(jnp.float32)).astype(jnp.bfloat16)
    start = table[3, 0] if late else 0
    end = table[4 if late else 3, 0]

    def products(first):
        values = []
        for k in range(0, GROUP, 2):
            left = [held[table[1, first + k + j]] for j in range(2)]
            right = [adjacency[table[2, first + k + j]] for j in range(2)]
            value = lax.dot_general(
                jnp.concatenate(left, axis=0),
                jnp.concatenate(right, axis=0),
                NT,
                preferred_element_type=jnp.float32,
            )
            rows = 2 * TILE
            values.append(value[:rows, :size] + value[rows : 2 * rows, :size])
            values.append(value[2 * rows : 3 * rows, size:] + value[3 * rows :, size:])
        return values

    def add(first, values):
        for k in range(GROUP):
            place = table[0, first + k]
            value = jnp.where(first + k < end, values[k], 0.0)
            out[place] += value[:TILE]
            out[place + CHIPS] += value[TILE:]

    def whole(i, before):
        after = products(start + i * GROUP)
        add(start + (i - 1) * GROUP, before)
        return after

    groups = (end - start + GROUP - 1) // GROUP
    last = lax.fori_loop(1, groups, whole, products(start))
    add(start + (jnp.maximum(groups, 1) - 1) * GROUP, last)


def early_kernel(table, own, paired, up, down, adjacency, out, held):
    out[...] = jnp.zeros_like(out)
    block_products(0, table, own, paired, up, down, adjacency, out, held)


def late_kernel(before, table, own, paired, up, down, adjacency, out, held):
    out[...] = before[...]
    block_products(1, table, own, paired, up, down, adjacency, out, held)


def blocks(before, lists, own, paired, stream, adjacency, target_blocks):
    slots, size, _ = adjacency.shape
    late = before is not None
    return pl.pallas_call(
        late_kernel if late else early_kernel,
        in_specs=[VMEM] * late + [SMEM] + [VMEM] * 5,
        out_specs=VMEM,
        out_shape=jax.ShapeDtypeStruct((2 * target_blocks, TILE, size), jnp.float32),
        scratch_shapes=[pltpu.VMEM((RUNS * own.shape[2] // size, 4 * TILE, size), jnp.bfloat16)],
        name="late_blocks" if late else "early_blocks",
        compiler_params=pltpu.CompilerParams(vmem_limit_bytes=8 * 2**20),
        cost_estimate=pl.CostEstimate(
            flops=4 * slots * size * size * UNITS,
            bytes_accessed=slots * size * size,
            transcendentals=0,
        ),
    )(*([before] if late else []), lists, own, paired, *stream, adjacency)


def combine_kernel(parts, out):
    size = parts.shape[3]
    low = lax.broadcasted_iota(jnp.int32, (TILE, size), 1) < T_DEV
    for chip in range(CHIPS):
        left, right = parts[0, chip], parts[0, CHIPS + chip]
        for n in range(1, parts.shape[0]):
            left += parts[n, chip]
            right += parts[n, CHIPS + chip]
        out[2 * chip] = jnp.where(low, left, pltpu.roll(right, T_DEV, 1))
        out[2 * chip + 1] = jnp.where(low, pltpu.roll(left, T_DEV, 1), right)


def combine(parts):
    return pl.pallas_call(
        combine_kernel,
        in_specs=[VMEM],
        out_specs=VMEM,
        out_shape=jax.ShapeDtypeStruct(parts.shape[1:], jnp.float32),
        name="combine",
        compiler_params=pltpu.CompilerParams(vmem_limit_bytes=4 * 2**20),
    )(parts)


def second_kernel(parts, bias_one, self_weight, neigh_weight, bias_two, seeds, neighbors, out):
    rows = []
    for k in range(parts.shape[0]):
        rows += [parts[k], pltpu.roll(parts[k], T_DEV, 1)]
    sums = jnp.concatenate(rows, axis=0)
    bias = jnp.broadcast_to(bias_one[...], (sums.shape[1], sums.shape[0])).T
    hidden = jnp.maximum(sums + bias, 0.0).astype(jnp.bfloat16)
    fan, count = neighbors.shape
    positions = lax.broadcasted_iota(jnp.int32, (hidden.shape[1], count), 0)
    pick_self = (positions == seeds[...]).astype(jnp.float32)
    tally = jnp.zeros(positions.shape, jnp.float32)
    for k in range(fan):
        tally += (positions == neighbors[k : k + 1]).astype(jnp.float32)
    picked = lax.dot_general(
        jnp.concatenate([pick_self.T, tally.T / fan], axis=0).astype(jnp.bfloat16),
        hidden,
        NT,
        preferred_element_type=jnp.float32,
    ).astype(jnp.bfloat16)
    out[...] = (
        lax.dot_general(
            picked[:count], self_weight[...], NT, preferred_element_type=jnp.float32
        )
        + lax.dot_general(
            picked[count:], neigh_weight[...], NT, preferred_element_type=jnp.float32
        )
        + bias_two[...]
    )


def second(parts, bias_one, self_weight, neigh_weight, bias_two, seeds, neighbors):
    return pl.pallas_call(
        second_kernel,
        in_specs=[VMEM] * 7,
        out_specs=VMEM,
        out_shape=jax.ShapeDtypeStruct((seeds.shape[0], bias_two.shape[0]), jnp.float32),
        name="second",
        compiler_params=pltpu.CompilerParams(vmem_limit_bytes=8 * 2**20),
    )(
        parts,
        bias_one[None, :],
        self_weight.T,
        neigh_weight.T,
        bias_two[None, :],
        seeds[None, :],
        neighbors.T,
    )


def on_device(
    features,
    adjacency,
    target_block,
    source_block,
    block_count,
    layer_one,
    bias_one,
    self_weight,
    neigh_weight,
    bias_two,
    seed_ids,
    neighbor_ids,
):
    size = adjacency.shape[1]
    node_count = lax.axis_size("node")
    feat_count = lax.axis_size("feat")
    target_blocks = T_DEV * node_count * feat_count // size

    pair = [(i, i ^ 1) for i in range(feat_count)]
    up = [(i, (i + 2) % feat_count) for i in range(feat_count)]
    down = [((i + 2) % feat_count, i) for i in range(feat_count)]

    def send(value, route):
        return lax.ppermute(value, "feat", route)

    tie = lax.optimization_barrier
    ordered = in_hop_order(layer_one)
    *opposite, own_first, own_second = project(True, ordered, features)
    opposite_own = own_first, own_second
    rest, rest_own = project(False, ordered, features)
    second_part = send(opposite[1], pair)
    first_part, rest = tie((send(opposite[0], pair), rest))
    opposite = first_part, second_part
    rest = send(rest, pair)

    order = block_count
    streams = []
    for own, other in zip(opposite_own, opposite):
        middle = own.shape[0] // 2
        onward = own[:middle] + other[:middle]
        back = own[middle:] + other[middle:]
        onward, back, order = tie((onward, back, order))
        streams.append((send(onward, up), send(back, down)))
    for turn in range(3):
        for k, (begin, end) in enumerate(SPANS):
            onward, back = streams[k]
            if turn == 0:
                zero = jnp.float32(0)
                onward = lax.pad(onward, zero, ((0, (end - begin) // 2, 0), (0, 0, 0), (0, 0, 0)))
                back = lax.pad(back, zero, (((end - begin) // 2, 0, 0), (0, 0, 0), (0, 0, 0)))
            rest, rest_own, order = tie((rest, rest_own, order))
            at = 2 * turn * UNITS
            onward = rest_own[at + begin : at + end] + rest[at + begin : at + end] + onward
            at += UNITS
            back = rest_own[at + begin : at + end] + rest[at + begin : at + end] + back
            onward, back, order = tie((onward, back, order))
            streams[k] = send(onward, up), send(back, down)

    early = SPANS[0][1] // 2 * (features.shape[0] // RUNS) // size
    lists = block_lists(target_block, source_block, block_count, early)
    partial = None
    for stream in streams:
        partial = blocks(partial, lists, rest_own, rest, stream, adjacency, target_blocks)

    partial = partial.reshape(node_count, 2 * CHIPS, TILE, size)
    parts = combine(lax.all_to_all(partial, "node", 0, 0))
    parts = lax.all_to_all(parts, "feat", 0, 0)
    return second(
        parts, bias_one, self_weight, neigh_weight, bias_two, seed_ids, neighbor_ids
    )


def solution(mesh):
    placed = (
        P("node", "feat"),
        P("node", None, None),
        P("node"),
        P("node"),
        P("node"),
        P("feat", None),
        P(),
        P(),
        P(),
        P(),
        P(("node", "feat")),
        P(("node", "feat"), None),
    )
    return jax.shard_map(
        on_device, mesh=mesh, in_specs=placed, out_specs=P(("node", "feat"), None), check_vma=False
    )
```

```python
import functools

import jax
import jax.numpy as jnp
from jax import lax
from jax.experimental import pallas as pl
from jax.experimental.pallas import tpu as pltpu
from jax.sharding import PartitionSpec as P

T_DEV = 64
CHIPS = 8
TILE = 8
RUNS = 8
SPANS = ((0, 10), (10, 16))
GROUP = 8
NT = (((1,), (1,)), ((), ()))
VMEM = pl.BlockSpec(memory_space=pltpu.VMEM)
SMEM = pl.BlockSpec(memory_space=pltpu.SMEM)

UNITS = 2 * RUNS


def project_kernel(ordered, features, *outs):
    lanes = outs[0].shape[2]
    tile = min(512, lanes)
    for i in range(features.shape[0] // tile):
        rows = features[i * tile : (i + 1) * tile]
        product = lax.dot_general(ordered[...], rows, NT, preferred_element_type=jnp.float32)
        run, at = divmod(i * tile, lanes)
        take = 0
        for out in outs:
            for k in range(out.shape[0] // RUNS):
                unit = k // 2 * UNITS + 2 * run + k % 2
                out[unit, :, at : at + tile] = product[take : take + TILE]
                take += TILE


def project(ordered, features):
    rows, columns = features.shape
    hidden = ordered.shape[0]
    shapes = [
        jax.ShapeDtypeStruct((strips * UNITS, TILE, rows // RUNS), jnp.float32)
        for strips in (1, CHIPS - 1)
    ] * 2
    return pl.pallas_call(
        project_kernel,
        in_specs=[VMEM] * 2,
        out_specs=[VMEM] * 4,
        out_shape=shapes,
        name="project",
        compiler_params=pltpu.CompilerParams(vmem_limit_bytes=8 * 2**20),
        cost_estimate=pl.CostEstimate(
            flops=2 * rows * columns * hidden,
            bytes_accessed=rows * columns * 2 + rows * hidden * 4,
            transcendentals=0,
        ),
    )(ordered, features)


def in_hop_order(layer_one):
    hidden = layer_one.shape[1]
    feat = lax.axis_index("feat")
    row = jnp.arange(hidden, dtype=jnp.int32)
    place = row % (hidden // 2) // (2 * TILE)
    hop = (place + 1) // 2
    hop = CHIPS // 2 + jnp.where(place % 2 == 1, -hop, hop)
    chip = ((feat >> 1) + hop) % CHIPS
    core = ((feat & 1) + (row < hidden // 2)) % 2
    wanted = (chip * 2 + core) * (2 * TILE) + row % (2 * TILE)
    pick = (jnp.arange(hidden, dtype=jnp.int32)[None, :] == wanted[:, None]).astype(jnp.bfloat16)
    return lax.dot_general(pick, layer_one, NT, preferred_element_type=jnp.float32).astype(
        jnp.bfloat16
    )


def lists_kernel(early, count, target, source, out):
    slots = target.shape[1]
    slot = lax.broadcasted_iota(jnp.int32, (1, slots), 1)
    late = (source[...] >= early).astype(jnp.int32)
    key = jnp.where(slot < count[0], late, 2) * slots + slot
    across = jnp.broadcast_to(key, (slots, slots))
    rank = jnp.sum((across.T < across).astype(jnp.float32), axis=0, keepdims=True)
    first = jnp.sum((key < slots).astype(jnp.float32), axis=1, keepdims=True)
    place = 2 * target[...] - target[...] % CHIPS
    row = lax.broadcasted_iota(jnp.int32, (out.shape[0], slots), 0)
    values = jnp.zeros(row.shape, jnp.float32)
    for k, value in enumerate((place, source[...], slot, first, count[0].astype(jnp.float32))):
        if k < 3:
            value = value.astype(jnp.float32)
        values = jnp.where(row == k, value, values)
    at = lax.broadcasted_iota(jnp.int32, (out.shape[1], slots), 0).astype(jnp.float32) == rank
    out[...] = lax.dot_general(
        values.astype(jnp.bfloat16),
        at.astype(jnp.bfloat16),
        NT,
        preferred_element_type=jnp.float32,
    ).astype(jnp.int32)


def block_lists(target_block, source_block, block_count, early):
    slots = target_block.shape[0]
    return pl.pallas_call(
        functools.partial(lists_kernel, early),
        in_specs=[SMEM] + [VMEM] * 2,
        out_specs=VMEM,
        out_shape=jax.ShapeDtypeStruct((TILE, slots + 128), jnp.int32),
        name="block_lists",
        compiler_params=pltpu.CompilerParams(vmem_limit_bytes=4 * 2**20),
    )(block_count, target_block[None, :], source_block[None, :])


def block_products(late, table, own, paired, up, down, adjacency, out, held):
    size = adjacency.shape[1]
    lanes = own.shape[2]
    base = own.shape[0] - UNITS
    begin = SPANS[late][0]
    for b in range(begin // 2 * lanes // size, SPANS[late][1] // 2 * lanes // size):
        run, at = divmod(b * size, lanes)
        at = slice(at, at + size)
        total = jnp.concatenate(
            [
                (own[base + unit, :, at] + paired[base + unit, :, at])
                + (up[unit - begin, :, at] + down[unit - begin, :, at])
                for unit in (2 * run, 2 * run + 1)
            ],
            axis=0,
        )
        upper = total.astype(jnp.bfloat16)
        held[b, : 2 * TILE] = upper
        held[b, 2 * TILE :] = (total - upper.astype(jnp.float32)).astype(jnp.bfloat16)
    start = table[3, 0] if late else 0
    end = table[4 if late else 3, 0]

    def products(first):
        values = []
        for k in range(0, GROUP, 2):
            left = [held[table[1, first + k + j]] for j in range(2)]
            right = [adjacency[table[2, first + k + j]] for j in range(2)]
            value = lax.dot_general(
                jnp.concatenate(left, axis=0),
                jnp.concatenate(right, axis=0),
                NT,
                preferred_element_type=jnp.float32,
            )
            rows = 2 * TILE
            values.append(value[:rows, :size] + value[rows : 2 * rows, :size])
            values.append(value[2 * rows : 3 * rows, size:] + value[3 * rows :, size:])
        return values

    def add(first, values):
        for k in range(GROUP):
            place = table[0, first + k]
            value = jnp.where(first + k < end, values[k], 0.0)
            out[place] += value[:TILE]
            out[place + CHIPS] += value[TILE:]

    def whole(i, before):
        after = products(start + i * GROUP)
        add(start + (i - 1) * GROUP, before)
        return after

    groups = (end - start + GROUP - 1) // GROUP
    last = lax.fori_loop(1, groups, whole, products(start))
    add(start + (jnp.maximum(groups, 1) - 1) * GROUP, last)


def early_kernel(table, own, paired, up, down, adjacency, out, held):
    out[...] = jnp.zeros_like(out)
    block_products(0, table, own, paired, up, down, adjacency, out, held)


def late_kernel(before, table, own, paired, up, down, adjacency, out, held):
    out[...] = before[...]
    block_products(1, table, own, paired, up, down, adjacency, out, held)


def blocks(before, lists, own, paired, stream, adjacency, target_blocks):
    slots, size, _ = adjacency.shape
    late = before is not None
    return pl.pallas_call(
        late_kernel if late else early_kernel,
        in_specs=[VMEM] * late + [SMEM] + [VMEM] * 5,
        out_specs=VMEM,
        out_shape=jax.ShapeDtypeStruct((2 * target_blocks, TILE, size), jnp.float32),
        scratch_shapes=[pltpu.VMEM((RUNS * own.shape[2] // size, 4 * TILE, size), jnp.bfloat16)],
        name="late_blocks" if late else "early_blocks",
        compiler_params=pltpu.CompilerParams(vmem_limit_bytes=8 * 2**20),
        cost_estimate=pl.CostEstimate(
            flops=4 * slots * size * size * UNITS,
            bytes_accessed=slots * size * size,
            transcendentals=0,
        ),
    )(*([before] if late else []), lists, own, paired, *stream, adjacency)


def combine_kernel(parts, out):
    size = parts.shape[3]
    low = lax.broadcasted_iota(jnp.int32, (TILE, size), 1) < T_DEV
    for chip in range(CHIPS):
        left, right = parts[0, chip], parts[0, CHIPS + chip]
        for n in range(1, parts.shape[0]):
            left += parts[n, chip]
            right += parts[n, CHIPS + chip]
        out[2 * chip] = jnp.where(low, left, pltpu.roll(right, T_DEV, 1))
        out[2 * chip + 1] = jnp.where(low, pltpu.roll(left, T_DEV, 1), right)


def combine(parts):
    return pl.pallas_call(
        combine_kernel,
        in_specs=[VMEM],
        out_specs=VMEM,
        out_shape=jax.ShapeDtypeStruct(parts.shape[1:], jnp.float32),
        name="combine",
        compiler_params=pltpu.CompilerParams(vmem_limit_bytes=4 * 2**20),
    )(parts)


def second_kernel(parts, bias_one, self_weight, neigh_weight, bias_two, seeds, neighbors, out):
    rows = []
    for k in range(parts.shape[0]):
        rows += [parts[k], pltpu.roll(parts[k], T_DEV, 1)]
    sums = jnp.concatenate(rows, axis=0)
    bias = jnp.broadcast_to(bias_one[...], (sums.shape[1], sums.shape[0])).T
    hidden = jnp.maximum(sums + bias, 0.0).astype(jnp.bfloat16)
    fan, count = neighbors.shape
    positions = lax.broadcasted_iota(jnp.int32, (hidden.shape[1], count), 0)
    pick_self = (positions == seeds[...]).astype(jnp.float32)
    tally = jnp.zeros(positions.shape, jnp.float32)
    for k in range(fan):
        tally += (positions == neighbors[k : k + 1]).astype(jnp.float32)
    picked = lax.dot_general(
        jnp.concatenate([pick_self.T, tally.T / fan], axis=0).astype(jnp.bfloat16),
        hidden,
        NT,
        preferred_element_type=jnp.float32,
    ).astype(jnp.bfloat16)
    out[...] = (
        lax.dot_general(
            picked[:count], self_weight[...], NT, preferred_element_type=jnp.float32
        )
        + lax.dot_general(
            picked[count:], neigh_weight[...], NT, preferred_element_type=jnp.float32
        )
        + bias_two[...]
    )


def second(parts, bias_one, self_weight, neigh_weight, bias_two, seeds, neighbors):
    return pl.pallas_call(
        second_kernel,
        in_specs=[VMEM] * 7,
        out_specs=VMEM,
        out_shape=jax.ShapeDtypeStruct((seeds.shape[0], bias_two.shape[0]), jnp.float32),
        name="second",
        compiler_params=pltpu.CompilerParams(vmem_limit_bytes=8 * 2**20),
    )(
        parts,
        bias_one[None, :],
        self_weight.T,
        neigh_weight.T,
        bias_two[None, :],
        seeds[None, :],
        neighbors.T,
    )


def on_device(
    features,
    adjacency,
    target_block,
    source_block,
    block_count,
    layer_one,
    bias_one,
    self_weight,
    neigh_weight,
    bias_two,
    seed_ids,
    neighbor_ids,
):
    size = adjacency.shape[1]
    node_count = lax.axis_size("node")
    feat_count = lax.axis_size("feat")
    target_blocks = T_DEV * node_count * feat_count // size

    pair = [(i, i ^ 1) for i in range(feat_count)]
    up = [(i, (i + 2) % feat_count) for i in range(feat_count)]
    down = [((i + 2) % feat_count, i) for i in range(feat_count)]

    def send(value, route):
        return lax.ppermute(value, "feat", route)

    tie = lax.optimization_barrier
    opposite, rest, opposite_own, rest_own = project(in_hop_order(layer_one), features)
    opposite, rest = tie((send(opposite, pair), rest))
    rest = send(rest, pair)

    order = block_count
    streams = []
    for begin, end in SPANS:
        middle = (end - begin) // 2
        opposite, opposite_own, order = tie((opposite, opposite_own, order))
        onward = opposite_own[begin : begin + middle] + opposite[begin : begin + middle]
        back = opposite_own[begin + middle : end] + opposite[begin + middle : end]
        onward, back, order = tie((onward, back, order))
        streams.append((send(onward, up), send(back, down)))
    for turn in range(3):
        for k, (begin, end) in enumerate(SPANS):
            onward, back = streams[k]
            if turn == 0:
                zero = jnp.float32(0)
                onward = lax.pad(onward, zero, ((0, (end - begin) // 2, 0), (0, 0, 0), (0, 0, 0)))
                back = lax.pad(back, zero, (((end - begin) // 2, 0, 0), (0, 0, 0), (0, 0, 0)))
            rest, rest_own, order = tie((rest, rest_own, order))
            at = 2 * turn * UNITS
            onward = rest_own[at + begin : at + end] + rest[at + begin : at + end] + onward
            at += UNITS
            back = rest_own[at + begin : at + end] + rest[at + begin : at + end] + back
            onward, back, order = tie((onward, back, order))
            streams[k] = send(onward, up), send(back, down)

    early = SPANS[0][1] // 2 * (features.shape[0] // RUNS) // size
    lists = block_lists(target_block, source_block, block_count, early)
    partial = None
    for stream in streams:
        partial = blocks(partial, lists, rest_own, rest, stream, adjacency, target_blocks)

    partial = partial.reshape(node_count, 2 * CHIPS, TILE, size)
    parts = combine(lax.all_to_all(partial, "node", 0, 0))
    parts = lax.all_to_all(parts, "feat", 0, 0)
    return second(
        parts, bias_one, self_weight, neigh_weight, bias_two, seed_ids, neighbor_ids
    )


def solution(mesh):
    placed = (
        P("node", "feat"),
        P("node", None, None),
        P("node"),
        P("node"),
        P("node"),
        P("feat", None),
        P(),
        P(),
        P(),
        P(),
        P(("node", "feat")),
        P(("node", "feat"), None),
    )
    return jax.shard_map(
        on_device, mesh=mesh, in_specs=placed, out_specs=P(("node", "feat"), None), check_vma=False
    )
```
